128 devices in a mesh: branch: 128 (over x, y, z, core).
Axes of the slice: x: 4, y: 4, z: 4, core: 2. Of those that a mesh axis runs over, the one named last changes fastest.
Arguments:
- points: float32 [3, 4194304], P(None, 'branch'), may hold values from 0 to 1
- charges: float32 [8, 4194304], P(None, 'branch'), may hold values from -6 to 6
- leaf_basis: bfloat16 [32768, 32, 128], P('branch'), may hold values from -0.5 to 0.5
- low_transfer: bfloat16 [65280, 1024], P('branch'), may hold values from -1 to 1
- low_coupling: bfloat16 [65408, 8, 1024], P('branch'), may hold values from -0.375 to 0.375
- low_partner: int32 [65408, 8], P('branch'), may hold values from -1 to 65407, as said below
- top_transfer: bfloat16 [252, 1024], replicated, may hold values from -1 to 1
- top_coupling: bfloat16 [126, 4, 1024], replicated, may hold values from -0.53033009 to 0.53033009
- top_partner: int32 [126, 4], replicated, may hold values from -1 to 63, as said below
- near_list: int32 [32768, 8], P('branch'), may hold values from -1 to 32767, as said below
Outputs:
- potential: float32 [8, 4194304], P(None, 'branch')
The draws below stay inside these ranges and needn't reach their ends.
Inputs may be any that keep to these rules, and one draw needn't show every extreme that they name: `low_partner`: row b * 511 + position lists coupling partners of that node of block b: each entry is -1 or the global id of another node of the same level k; numbering the nodes of level k of all blocks end to end (block by block), the partner's number differs from the node's own by 1 to max(1, 64 / 2^k) (integer division). The first entry is never -1. `top_partner`: each entry is -1 or the index, within its level, of another node of the same level; the first entry is never -1. `near_list`: entry 0 of leaf g's list is g; every other entry is -1 or a leaf within 64 leaves of g.
All inputs are finite; a program needn't handle non-finite values.
Results may differ from the reference program's by a relative error of at most 0.004.
Values sent between devices are 32-bit elements; how exact they have to be, the bound alone decides.
A program may use at most 256 MiB of HBM per device.

```python
import math
import jax
import jax.numpy as jnp
from jax import lax

LEAF_DEV = 256
LEAF = 128
RANK = 32
RHS = 8
KL = 8
KT = 4
NK = 8
LOWN = 510
LEAVES = 32768
NPTS = 4194304
TOPN = 252
TOPC = 126
N_BRANCH = 128


def level_of(position, total, depth_count):
    found = jnp.zeros_like(position)
    for depth_at in range(1, depth_count + 1):
        found = found + (position >= 2 * total - (2 * total >> depth_at)).astype(jnp.int32)
    return found


def coupling_values(key, shape_all, spread):
    values = jnp.clip(jax.random.normal(key, shape_all, jnp.float32), -6.0, 6.0)
    return values * spread[:, None, None]


def draw_low_coupling(key, part):
    key = jax.random.fold_in(key, 11)
    depth_low = LEAF_DEV.bit_length() - 1
    nodes_dev = 2 * LEAF_DEV - 1
    total_rows = N_BRANCH * nodes_dev
    position = jnp.arange(total_rows, dtype=jnp.int32) % nodes_dev
    found = level_of(position, LEAF_DEV, depth_low).astype(jnp.float32)
    spread = jnp.exp2(-0.5 * found) / math.sqrt(RANK * KL)
    return coupling_values(key, (total_rows, KL, RANK * RANK), spread).astype(jnp.bfloat16)


def draw_top_coupling(key, part):
    key = jax.random.fold_in(key, 12)
    depth_low = LEAF_DEV.bit_length() - 1
    depth_top = N_BRANCH.bit_length() - 1
    total_rows = N_BRANCH - 2
    row_ids = jnp.arange(total_rows, dtype=jnp.int32)
    found = jnp.ones_like(row_ids)
    for depth_at in range(2, depth_top):
        found = found + (row_ids >= N_BRANCH - (2 * N_BRANCH >> depth_at)).astype(jnp.int32)
    spread = jnp.exp2(-0.5 * (found + depth_low).astype(jnp.float32)) / math.sqrt(RANK * KT)
    return coupling_values(key, (total_rows, KT, RANK * RANK), spread).astype(jnp.bfloat16)


def draw_low_partner(key, part):
    key = jax.random.fold_in(key, 13)
    depth_low = LEAF_DEV.bit_length() - 1
    nodes_dev = 2 * LEAF_DEV - 1
    total_rows = N_BRANCH * nodes_dev
    row_ids = jnp.arange(total_rows, dtype=jnp.int32)
    block_id = row_ids // nodes_dev
    position = row_ids % nodes_dev
    found = level_of(position, LEAF_DEV, depth_low)
    offset = 2 * LEAF_DEV - jnp.right_shift(2 * LEAF_DEV, found)
    width_now = jnp.right_shift(LEAF_DEV, found)
    spot = block_id * width_now + position - offset
    reach_now = jnp.maximum(1, jnp.right_shift(LEAF_DEV // 4, found))
    first_key, second_key, third_key = jax.random.split(key, 3)
    stride = jax.random.randint(first_key, (total_rows, KL), 1, reach_now[:, None] + 1)
    signs = 2 * jax.random.randint(second_key, (total_rows, KL), 0, 2) - 1
    target = spot[:, None] + signs * stride
    first_pick = jnp.where(spot + stride[:, 0] < N_BRANCH * width_now, spot + stride[:, 0], spot - stride[:, 0])
    target = target.at[:, 0].set(first_pick)
    keeping = jax.random.randint(third_key, (total_rows, KL), 0, 4) > 0
    keeping = keeping.at[:, 0].set(True)
    limit = (N_BRANCH * width_now)[:, None]
    usable = keeping & (target >= 0) & (target < limit)
    safe_target = jnp.clip(target, 0, limit - 1)
    ident = safe_target // width_now[:, None] * nodes_dev + offset[:, None] + safe_target % width_now[:, None]
    result = jnp.where(usable, ident, -1)
    return result.at[0, KL - 1].set(-1).astype(jnp.int32)


def draw_top_partner(key, part):
    key = jax.random.fold_in(key, 14)
    depth_top = N_BRANCH.bit_length() - 1
    total_rows = N_BRANCH - 2
    row_ids = jnp.arange(total_rows, dtype=jnp.int32)
    found = jnp.ones_like(row_ids)
    for depth_at in range(2, depth_top):
        found = found + (row_ids >= N_BRANCH - (2 * N_BRANCH >> depth_at)).astype(jnp.int32)
    start = N_BRANCH - jnp.right_shift(2 * N_BRANCH, found)
    width_now = jnp.right_shift(N_BRANCH, found)
    inside = row_ids - start
    first_key, second_key = jax.random.split(key, 2)
    jump = jax.random.randint(first_key, (total_rows, KT), 0, (width_now - 1)[:, None])
    others = (inside[:, None] + 1 + jump) % width_now[:, None]
    others = others.at[:, 0].set((inside + width_now // 2) % width_now)
    keeping = jax.random.randint(second_key, (total_rows, KT), 0, 4) > 0
    keeping = keeping.at[:, 0].set(True)
    result = jnp.where(keeping, others, -1)
    return result.at[0, KT - 1].set(-1).astype(jnp.int32)


def draw_near_list(key, part):
    key = jax.random.fold_in(key, 15)
    leaf_total = N_BRANCH * LEAF_DEV
    reach_now = LEAF_DEV // 4
    first_key, second_key, third_key, fourth_key = jax.random.split(key, 4)
    row_ids = jnp.arange(leaf_total, dtype=jnp.int32)
    busy = jax.random.randint(first_key, (N_BRANCH,), 1, 5)[row_ids // LEAF_DEV]
    stride = jax.random.randint(second_key, (leaf_total, NK), 1, reach_now + 1)
    signs = 2 * jax.random.randint(third_key, (leaf_total, NK), 0, 2) - 1
    target = row_ids[:, None] + signs * stride
    keeping = jax.random.randint(fourth_key, (leaf_total, NK), 0, 4) < busy[:, None]
    usable = keeping & (target >= 0) & (target < leaf_total)
    result = jnp.where(usable, target, -1)
    result = result.at[:, 0].set(row_ids)
    return result.at[0, 1].set(-1).astype(jnp.int32)


def steps_of(rng, extent, shards, low, top_value):
    def one(dim, shards_of):
        draws = jax.random.uniform(jax.random.fold_in(jax.random.fold_in(rng, 6), dim), (shards_of,), jnp.float32, low / len(shards), top_value / len(shards))
        return jnp.repeat(jnp.exp(draws), extent[dim] // shards_of).reshape((-1,) + (1,) * (len(extent) - dim - 1))

    factor_of = one(*shards[0])
    for cut in shards[1:]:
        factor_of = factor_of * one(*cut)
    return factor_of


def gaussian(stream_key, extent, deviation, most, pieces=(), held_as=jnp.bfloat16):
    values = deviation * jax.random.normal(stream_key, extent, jnp.float32)
    if pieces:
        values = values * steps_of(stream_key, extent, pieces, -0.22, 0.18)
    return jnp.clip(values, -most, most).astype(held_as)


def setup_inputs(seed: int = 0) -> dict:
    key_list = jax.random.split(jax.random.key(seed), 11)
    points = jnp.clip(1.0 * jax.random.uniform(key_list[0], (3, NPTS), jnp.float32) ** steps_of(key_list[0], (3, NPTS), ((1, 128),), -0.2, 0.2), 0.0, 1.0)
    charges = gaussian(key_list[1], (RHS, NPTS), 1.0, 6.0, ((1, 128),), jnp.float32)
    leaf_basis = gaussian(key_list[2], (LEAVES, RANK, LEAF), LEAF ** -0.5, 0.5, ((0, 128),))
    low_transfer = gaussian(key_list[3], (N_BRANCH * LOWN, RANK * RANK), RANK ** -0.5, 1.0, ((0, 128),))
    low_coupling = draw_low_coupling(jax.random.fold_in(key_list[10], 71), 0)
    low_partner = draw_low_partner(jax.random.fold_in(key_list[10], 71), 0)
    top_transfer = gaussian(key_list[6], (TOPN, RANK * RANK), RANK ** -0.5, 1.0)
    top_coupling = draw_top_coupling(jax.random.fold_in(key_list[10], 71), 0)
    top_partner = draw_top_partner(jax.random.fold_in(key_list[10], 71), 0)
    near_list = draw_near_list(jax.random.fold_in(key_list[10], 71), 0)
    return dict(points=points, charges=charges, leaf_basis=leaf_basis, low_transfer=low_transfer, low_coupling=low_coupling, low_partner=low_partner, top_transfer=top_transfer, top_coupling=top_coupling, top_partner=top_partner, near_list=near_list)


SOFTEN = 0.0025
KERNEL_SCALE = 1.0 / (4.0 * math.pi)
HIGH = lax.Precision.HIGHEST

def level_start(total, depth_at):
    return 2 * total - (2 * total >> depth_at)

def kernel_tiles(targets, picked, valid):
    square = None
    for axis_id in range(3):
        gap = targets[:, None, axis_id, :, None] - picked[:, :, axis_id, None, :]
        square = gap * gap if axis_id == 0 else square + gap * gap
    tiles = KERNEL_SCALE * lax.rsqrt(square + SOFTEN) * valid[:, :, None, None]
    return tiles.astype(jnp.bfloat16)

def reference(points, charges, leaf_basis, low_transfer, low_coupling, low_partner, top_transfer, top_coupling, top_partner, near_list):
    depth_low = LEAF_DEV.bit_length() - 1
    depth_top = N_BRANCH.bit_length() - 1
    nodes_dev = 2 * LEAF_DEV - 1
    lower_dev = 2 * LEAF_DEV - 2
    rounded = charges.astype(jnp.bfloat16)
    leaf_loads = rounded.reshape(RHS, LEAVES, LEAF).transpose(1, 0, 2)
    leaf_points = points.reshape(3, LEAVES, LEAF).transpose(1, 0, 2)
    basis = leaf_basis.astype(jnp.float32)
    coef_leaf = jnp.einsum('lrp,lkp->lrk', basis, leaf_loads.astype(jnp.float32), precision=HIGH)
    transfer = low_transfer.astype(jnp.float32).reshape(N_BRANCH, lower_dev, RANK, RANK)
    levels_up = [coef_leaf.reshape(N_BRANCH, LEAF_DEV, RANK, RHS)]
    for depth_at in range(depth_low):
        start = level_start(LEAF_DEV, depth_at)
        width_now = LEAF_DEV >> depth_at
        moved = jnp.einsum('dmab,dmak->dmbk', transfer[:, start:start + width_now], levels_up[-1], precision=HIGH)
        levels_up.append(moved[:, 0::2] + moved[:, 1::2])
    coef_low = jnp.concatenate(levels_up, axis=1).reshape(N_BRANCH * nodes_dev, RANK, RHS)
    coupling = low_coupling.reshape(N_BRANCH, nodes_dev, KL, RANK, RANK)
    partners = low_partner.reshape(N_BRANCH, nodes_dev, KL)

    def couple_block(pair):
        partner_rows, matrices = pair
        present = (partner_rows >= 0).astype(jnp.float32)
        picked = coef_low[jnp.maximum(partner_rows, 0)] * present[..., None, None]
        return jnp.einsum('nsab,nsbk->nak', matrices.astype(jnp.float32), picked, precision=HIGH)
    far_low = lax.map(couple_block, (partners, coupling))
    top_moves = top_transfer.astype(jnp.float32).reshape(TOPN, RANK, RANK)
    top_mats = top_coupling.astype(jnp.float32).reshape(TOPC, KT, RANK, RANK)
    uppers = [levels_up[-1][:, 0]]
    for depth_at in range(depth_top - 1):
        start = level_start(N_BRANCH, depth_at)
        width_now = N_BRANCH >> depth_at
        moved = jnp.einsum('mab,mak->mbk', top_moves[start:start + width_now], uppers[-1], precision=HIGH)
        uppers.append(moved[0::2] + moved[1::2])
    far_top = [None]
    for depth_at in range(1, depth_top):
        start = level_start(N_BRANCH, depth_at) - N_BRANCH
        width_now = N_BRANCH >> depth_at
        rows_now = top_partner[start:start + width_now]
        present = (rows_now >= 0).astype(jnp.float32)
        picked = uppers[depth_at][jnp.maximum(rows_now, 0)] * present[..., None, None]
        far_top.append(jnp.einsum('msab,msbk->mak', top_mats[start:start + width_now], picked, precision=HIGH))
    downward = far_top[depth_top - 1]
    for depth_at in range(depth_top - 2, 0, -1):
        start = level_start(N_BRANCH, depth_at)
        width_now = N_BRANCH >> depth_at
        downward = far_top[depth_at] + jnp.einsum('mab,mbk->mak', top_moves[start:start + width_now], jnp.repeat(downward, 2, axis=0), precision=HIGH)
    downward = far_low[:, nodes_dev - 1] + jnp.einsum('mab,mbk->mak', top_moves[:N_BRANCH], jnp.repeat(downward, 2, axis=0), precision=HIGH)
    downward = downward[:, None]
    for depth_at in range(depth_low - 1, -1, -1):
        start = level_start(LEAF_DEV, depth_at)
        width_now = LEAF_DEV >> depth_at
        downward = far_low[:, start:start + width_now] + jnp.einsum('dmab,dmbk->dmak', transfer[:, start:start + width_now], jnp.repeat(downward, 2, axis=1), precision=HIGH)
    leaf_coef = downward.reshape(LEAVES, RANK, RHS).astype(jnp.bfloat16)
    far_field = jnp.einsum('lrp,lrk->lkp', basis, leaf_coef.astype(jnp.float32), precision=HIGH)
    block_size = min(16, LEAF_DEV)
    count_blocks = LEAVES // block_size

    def near_block(pack):
        targets, index = pack
        present = (index >= 0).astype(jnp.float32)
        safe = jnp.maximum(index, 0)
        tiles = kernel_tiles(targets, leaf_points[safe], present)
        return jnp.einsum('bkts,bkrs->brt', tiles.astype(jnp.float32), leaf_loads[safe].astype(jnp.float32), precision=HIGH)
    near_field = lax.map(near_block, (leaf_points.reshape(count_blocks, block_size, 3, LEAF), near_list.reshape(count_blocks, block_size, NK)))
    near_field = near_field.reshape(LEAVES, RHS, LEAF)
    total = far_field + near_field
    return total.transpose(1, 0, 2).reshape(RHS, NPTS)
```

```python
import math

import jax
import jax.numpy as jnp
from jax import lax
from jax.experimental import pallas as pl
from jax.experimental.pallas import tpu as pltpu
from jax.sharding import PartitionSpec as P

SOFTEN = 0.0025
FOURPI = 4.0 * math.pi
F32 = jnp.float32
BF16 = jnp.bfloat16
VMEM_BYTES = 56 << 20


def level_start(total, depth_at):
    return 2 * total - (2 * total >> depth_at)


def halo_counts(leaves, depth):
    return [max(1, (leaves // 4) >> k) for k in range(depth + 1)]


def lane_group(shape):
    return lax.broadcasted_iota(jnp.int32, shape, len(shape) - 1) // 32


def spread_groups(z):
    z = z + pltpu.roll(z, 32, axis=z.ndim - 1)
    return z + pltpu.roll(z, 64, axis=z.ndim - 1)


def expand_matrix():
    r = lax.broadcasted_iota(jnp.int32, (128, 1024), 0)
    c = lax.broadcasted_iota(jnp.int32, (128, 1024), 1)
    return jnp.where(((r % 32) == (c // 32)) & (r < 96), 1.0, 0.0).astype(BF16)


def reduce_matrix():
    r = lax.broadcasted_iota(jnp.int32, (1024, 128), 0)
    c = lax.broadcasted_iota(jnp.int32, (1024, 128), 1)
    return jnp.where((r // 32) == (c % 32), 1.0, 0.0).astype(BF16)


def expand(u, xmat):
    hi = u.astype(BF16).astype(F32)
    rest = u - hi
    mid = rest.astype(BF16).astype(F32)
    low = rest - mid
    group = lane_group(u.shape)
    parts = jnp.where(group == 0, hi, jnp.where(group == 1, mid, jnp.where(group == 2, low, 0.0)))
    return jnp.dot(parts.astype(BF16), xmat, preferred_element_type=F32)


def reduce32(acc, rmat):
    hi = acc.astype(BF16)
    low = (acc - hi.astype(F32)).astype(BF16)
    return jnp.dot(hi, rmat, preferred_element_type=F32) + jnp.dot(
        low, rmat, preferred_element_type=F32
    )


def move_up(u_ref, e_ref, xmat_ref, src, dst, e_row, width):
    group = min(16, width)

    def step(i, carry):
        first = i * group
        u = u_ref[pl.ds(src + first, group)].reshape(group * 8, 128)
        wide = expand(u, xmat_ref[...])
        for n in range(0, group, 2):
            total = None
            for m in (n, n + 1):
                row = e_ref[pl.ds(e_row + first + m, 1), :]
                prod = wide[8 * m : 8 * m + 8] * row
                for j in range(8):
                    piece = prod[:, 128 * j : 128 * j + 128]
                    total = piece if total is None else total + piece
            u_ref[dst + i * (group // 2) + n // 2] = spread_groups(total)
        return carry

    if width == group:
        step(0, 0)
    else:
        lax.fori_loop(0, width // group, step, 0)


def upcast_rows(dst_ref, src_ref, rows):
    for first in range(0, rows, 64):
        count = min(64, rows - first)
        dst_ref[first : first + count, :] = src_ref[first : first + count, :].astype(F32)


def make_upward(leaves):
    depth = leaves.bit_length() - 1
    counts = halo_counts(leaves, depth)

    def kernel(charges_ref, basis_ref, transfer_ref, u_ref, last_ref, first_ref, e_ref, xmat_ref):
        xmat_ref[...] = expand_matrix()
        upcast_rows(e_ref, transfer_ref, 2 * leaves - 2)

        def leaf_step(i, carry):
            at = pl.multiple_of(i * 1024, 1024)
            loads = charges_ref[:, pl.ds(at, 1024)]
            loads = jnp.concatenate([loads[:, 128 * g : 128 * g + 128] for g in range(8)], axis=0)
            basis = basis_ref[pl.ds(pl.multiple_of(i * 256, 256), 256), :]
            out = lax.dot_general(
                loads.astype(BF16), basis, (((1,), (1,)), ((), ())), preferred_element_type=F32
            )
            group = lane_group((8, 128))
            for g in range(8):
                piece = out[8 * g : 8 * g + 8, 128 * (g // 4) : 128 * (g // 4) + 128]
                u_ref[i * 8 + g] = spread_groups(jnp.where(group == g % 4, piece, 0.0))
            return carry

        lax.fori_loop(0, leaves // 8, leaf_step, 0)
        for k in range(depth):
            src = level_start(leaves, k)
            move_up(u_ref, e_ref, xmat_ref, src, level_start(leaves, k + 1), src, leaves >> k)

        for out_ref, tail in ((last_ref, True), (first_ref, False)):
            nodes = []
            for k in range(depth + 1):
                start, width = level_start(leaves, k), leaves >> k
                begin = start + width - counts[k] if tail else start
                nodes += list(range(begin, begin + counts[k]))
            group = lane_group((8, 128))
            for at in range(0, len(nodes), 4):
                four = nodes[at : at + 4]
                packed = u_ref[four[0]]
                for g in range(1, len(four)):
                    packed = jnp.where(group == g, u_ref[four[g]], packed)
                out_ref[at // 4] = packed

    packs = -(-sum(counts) // 4)
    rows = 2 * leaves - 1
    return pl.pallas_call(
        kernel,
        out_shape=(
            jax.ShapeDtypeStruct((rows, 8, 128), F32),
            jax.ShapeDtypeStruct((packs, 8, 128), F32),
            jax.ShapeDtypeStruct((packs, 8, 128), F32),
        ),
        in_specs=[pl.BlockSpec(memory_space=pltpu.VMEM)] * 3,
        out_specs=(pl.BlockSpec(memory_space=pltpu.VMEM),) * 3,
        scratch_shapes=[pltpu.VMEM((rows - 1, 1024), F32), pltpu.VMEM((128, 1024), BF16)],
        compiler_params=pltpu.CompilerParams(vmem_limit_bytes=VMEM_BYTES),
        cost_estimate=pl.CostEstimate(flops=10**9, bytes_accessed=6 << 20, transcendentals=0),
        name="upward",
    )


def point_rows(points):
    n = points.shape[1]
    row = lax.broadcasted_iota(jnp.int32, (8, n), 0)
    scaled = (points - 0.5) * FOURPI
    value = jnp.where(
        row == 0, scaled[0:1], jnp.where(row == 1, scaled[1:2], jnp.where(row == 2, scaled[2:3], 0.0))
    )
    high = value.astype(BF16).astype(F32)
    low = (value - high).astype(BF16).astype(F32)
    both = high + low
    norm = jnp.sum(both * both, axis=0, keepdims=True)
    return row, high, low, norm


def three_parts(norm):
    one = norm.astype(BF16).astype(F32)
    rest = norm - one
    two = rest.astype(BF16).astype(F32)
    return one, two, rest - two


def source_rows(row, high, low, norm):
    m1, m2, m3 = three_parts(norm)
    unit = row == 4
    s0 = jnp.where(row == 3, m1, jnp.where(unit, 1.0, high))
    s1 = jnp.where(row == 3, m2, jnp.where(unit, 1.0, low))
    s2 = jnp.where(row == 3, m3, jnp.where(unit, 1.0, high))
    return jnp.concatenate([s0, s1, s2, low], axis=0).astype(BF16)


def target_rows(row, high, low, norm):
    n1, n2, n3 = three_parts(norm + SOFTEN * FOURPI * FOURPI)
    unit = row == 3
    t0 = jnp.where(row == 4, n1, jnp.where(unit, 1.0, -2.0 * high))
    t1 = jnp.where(row == 4, n2, jnp.where(unit, 1.0, -2.0 * high))
    t2 = jnp.where(row == 4, n3, jnp.where(unit, 1.0, -2.0 * low))
    return jnp.concatenate([t0, t1, t2, -2.0 * low], axis=0).astype(BF16)


def make_near(leaves, slots):
    reach = leaves // 4
    span = leaves + 2 * reach
    unroll = 4
    wide = slots * 128

    def kernel(
        index_ref,
        pts_ref,
        pts_before_ref,
        pts_after_ref,
        chg_ref,
        chg_before_ref,
        chg_after_ref,
        out_ref,
        src_ref,
        tgt_ref,
        load_ref,
        tile_ref,
        rhs_ref,
    ):
        def prepare(points, charges, first, own_first, i):
            at = pl.multiple_of(i * 1024, 1024)
            rows = point_rows(points[:, pl.ds(at, 1024)])
            source = source_rows(*rows)
            loads = charges[:, pl.ds(at, 1024)]
            for g in range(8):
                src_ref[first + i * 8 + g] = source[:, 128 * g : 128 * g + 128]
                load_ref[first + i * 8 + g] = loads[:, 128 * g : 128 * g + 128]
            if own_first is not None:
                target = target_rows(*rows)
                for g in range(8):
                    tgt_ref[i * 8 + g] = target[:, 128 * g : 128 * g + 128]

        def run(points, charges, first, own_first, count):
            def step(i, carry):
                prepare(points, charges, first, own_first, i)
                return carry

            lax.fori_loop(0, count // 8, step, 0)

        run(pts_before_ref, chg_before_ref, 0, None, reach)
        run(pts_ref, chg_ref, reach, 0, leaves)
        run(pts_after_ref, chg_after_ref, reach + leaves, None, reach)
        src_ref[span] = src_ref[reach]
        load_ref[span] = jnp.zeros((8, 128), F32)

        def tiles_of(leaf, slot, j):
            target = tgt_ref[leaf]
            for s in range(slots):
                q = index_ref[leaf * slots + s]
                square = lax.dot_general(
                    src_ref[q], target, (((0,), (0,)), ((), ())), preferred_element_type=F32
                )
                tile_ref[slot, j, 128 * s : 128 * s + 128, :] = lax.rsqrt(square).astype(BF16)
                rhs_ref[slot, j, :, 128 * s : 128 * s + 128] = load_ref[q]

        def apply(leaf, slot, j):
            at = pl.multiple_of(leaf * 128, 128)
            out_ref[:, pl.ds(at, 128)] = jnp.dot(
                rhs_ref[slot, j].astype(BF16), tile_ref[slot, j], preferred_element_type=F32
            )

        for j in range(unroll):
            tiles_of(j, 0, j)

        def step(i, carry):
            for half in range(2):
                base = (2 * i + half) * unroll
                for j in range(unroll):
                    tiles_of(jnp.minimum(base + unroll + j, leaves - 1), 1 - half, j)
                for j in range(unroll):
                    apply(base + j, half, j)
            return carry

        lax.fori_loop(0, leaves // (2 * unroll), step, 0)

    return pl.pallas_call(
        kernel,
        out_shape=jax.ShapeDtypeStruct((8, leaves * 128), F32),
        in_specs=[pl.BlockSpec(memory_space=pltpu.SMEM)]
        + [pl.BlockSpec(memory_space=pltpu.VMEM)] * 6,
        out_specs=pl.BlockSpec(memory_space=pltpu.VMEM),
        scratch_shapes=[
            pltpu.VMEM((span + 1, 32, 128), BF16),
            pltpu.VMEM((leaves, 32, 128), BF16),
            pltpu.VMEM((span + 1, 8, 128), F32),
            pltpu.VMEM((2, unroll, wide, 128), BF16),
            pltpu.VMEM((2, unroll, 8, wide), F32),
        ],
        compiler_params=pltpu.CompilerParams(vmem_limit_bytes=VMEM_BYTES),
        cost_estimate=pl.CostEstimate(
            flops=3 * 10**10, bytes_accessed=8 << 20, transcendentals=leaves * slots * 128 * 128
        ),
        name="near",
    )


def make_far(leaves, branches, slots, top_slots):
    depth = leaves.bit_length() - 1
    depth_top = branches.bit_length() - 1
    counts = halo_counts(leaves, depth)
    rows = 2 * leaves - 1
    chunk = 64
    steps = -(-rows // chunk)
    top_rows = 2 * branches - 4

    def kernel(
        me_ref,
        partner_ref,
        top_partner_ref,
        u_ref,
        before_ref,
        after_ref,
        roots_ref,
        coupling_ref,
        transfer_ref,
        top_transfer_ref,
        top_coupling_ref,
        basis_ref,
        near_ref,
        out_ref,
        table_ref,
        far_ref,
        e_ref,
        top_e_ref,
        c_ref,
        acc_ref,
        upper_ref,
        xmat_ref,
        rmat_ref,
    ):
        step_id = pl.program_id(0)

        @pl.when(step_id == 0)
        def _():
            xmat_ref[...] = expand_matrix()
            rmat_ref[...] = reduce_matrix()
            table_ref[rows : 2 * rows] = u_ref[...]
            table_ref[3 * rows] = jnp.zeros((8, 128), F32)
            group = lane_group((8, 128))
            for in_ref, tail, base in ((before_ref, True, 0), (after_ref, False, 2 * rows)):
                at = 0
                for k in range(depth + 1):
                    start, width = level_start(leaves, k), leaves >> k
                    begin = base + (start + width - counts[k] if tail else start)
                    if counts[k] >= 4:

                        def unpack(i, carry, in_ref=in_ref, at=at, begin=begin):
                            packed = in_ref[at // 4 + i]
                            for g in range(4):
                                table_ref[begin + 4 * i + g] = spread_groups(
                                    jnp.where(group == g, packed, 0.0)
                                )
                            return carry

                        lax.fori_loop(0, counts[k] // 4, unpack, 0)
                    else:
                        for i in range(counts[k]):
                            packed = in_ref[(at + i) // 4]
                            table_ref[begin + i] = spread_groups(
                                jnp.where(group == (at + i) % 4, packed, 0.0)
                            )
                    at += counts[k]

        def couple(sub, carry):
            first = sub * 16
            c_ref[...] = coupling_ref[pl.ds(first, 16)].reshape(16 * slots, 1024).astype(F32)

            def four(i, carry):
                for m in range(4):
                    n = 4 * i + m
                    node = jnp.minimum(step_id * chunk + first + n, rows - 1)
                    acc = [None] * 8
                    for s in range(slots):
                        u = table_ref[partner_ref[node * slots + s]]
                        row = c_ref[pl.ds(n * slots + s, 1), :]
                        for j in range(8):
                            piece = u * row[:, 128 * j : 128 * j + 128]
                            acc[j] = piece if acc[j] is None else acc[j] + piece
                    for j in range(8):
                        acc_ref[pl.ds(pl.multiple_of(n * 8, 8), 8), 128 * j : 128 * j + 128] = acc[j]
                return carry

            lax.fori_loop(0, 4, four, 0)
            far = reduce32(acc_ref[...], rmat_ref[...])
            far_ref[pl.ds(step_id * chunk + first, 16)] = far.reshape(16, 8, 128)
            return carry

        lax.fori_loop(0, chunk // 16, couple, 0)

        @pl.when(step_id == steps - 1)
        def _():
            me = me_ref[0]
            upcast_rows(e_ref, transfer_ref, rows - 1)
            upcast_rows(top_e_ref, top_transfer_ref, top_rows)
            upper_ref[0:branches] = roots_ref[...]
            for u in range(depth_top - 1):
                src = level_start(branches, u)
                move_up(
                    upper_ref, top_e_ref, xmat_ref, src, level_start(branches, u + 1), src, branches >> u
                )
            upper_ref[2 * branches - 2] = jnp.zeros((8, 128), F32)
            for u in range(1, depth_top):
                row_at = level_start(branches, u) - branches + (me >> u)
                mats = top_coupling_ref[row_at].astype(F32)
                acc = [None] * 8
                for s in range(top_slots):
                    entry = top_partner_ref[row_at * top_slots + s]
                    at = jnp.where(entry >= 0, level_start(branches, u) + entry, 2 * branches - 2)
                    value = upper_ref[at]
                    for j in range(8):
                        piece = value * mats[s : s + 1, 128 * j : 128 * j + 128]
                        acc[j] = piece if acc[j] is None else acc[j] + piece
                for j in range(8):
                    acc_ref[8 * u - 8 : 8 * u, 128 * j : 128 * j + 128] = acc[j]
            far_top = reduce32(acc_ref[0 : 8 * (depth_top - 1)], rmat_ref[...])

            def down(value, row):
                wide = jnp.concatenate([value] * 8, axis=1) * row
                return reduce32(wide, rmat_ref[...])

            current = far_top[8 * (depth_top - 2) :]
            for u in range(depth_top - 2, 0, -1):
                row = top_e_ref[pl.ds(level_start(branches, u) + (me >> u), 1), :]
                current = far_top[8 * u - 8 : 8 * u] + down(current, row)
            row = top_e_ref[pl.ds(me, 1), :]
            far_ref[rows - 1] = far_ref[rows - 1] + down(current, row)
            for k in range(depth - 1, -1, -1):
                start, width = level_start(leaves, k), leaves >> k
                parents = level_start(leaves, k + 1)
                size = min(16, width)

                def level(i, carry, start=start, parents=parents, size=size):
                    for n in range(size):
                        value = far_ref[parents + i * (size // 2) + n // 2]
                        row = e_ref[pl.ds(start + i * size + n, 1), :]
                        for j in range(8):
                            acc_ref[8 * n : 8 * n + 8, 128 * j : 128 * j + 128] = (
                                value * row[:, 128 * j : 128 * j + 128]
                            )
                    moved = reduce32(acc_ref[0 : 8 * size], rmat_ref[...])
                    at = pl.ds(start + i * size, size)
                    far_ref[at] = far_ref[at] + moved.reshape(size, 8, 128)
                    return carry

                if width == size:
                    level(0, 0)
                else:
                    lax.fori_loop(0, width // size, level, 0)

            def leaf_step(i, carry):
                group = lane_group((8, 128))
                pieces = []
                for g in range(8):
                    coef = far_ref[i * 8 + g]
                    only = jnp.where(group == g % 4, coef, 0.0)
                    none = jnp.zeros((8, 128), F32)
                    pieces.append(jnp.concatenate([only, none] if g < 4 else [none, only], axis=1))
                coefs = jnp.concatenate(pieces, axis=0).astype(BF16)
                basis = basis_ref[pl.ds(pl.multiple_of(i * 256, 256), 256), :]
                values = jnp.dot(coefs, basis, preferred_element_type=F32)
                for g in range(8):
                    at = pl.ds(pl.multiple_of((i * 8 + g) * 128, 128), 128)
                    out_ref[:, at] = near_ref[:, at] + values[8 * g : 8 * g + 8]
                return carry

            lax.fori_loop(0, leaves // 8, leaf_step, 0)

    smem = pl.BlockSpec(memory_space=pltpu.SMEM)
    vmem = pl.BlockSpec(memory_space=pltpu.VMEM)
    return pl.pallas_call(
        kernel,
        grid=(steps,),
        out_shape=jax.ShapeDtypeStruct((8, leaves * 128), F32),
        in_specs=[smem] * 3
        + [vmem] * 4
        + [pl.BlockSpec((chunk, slots, 1024), lambda i: (i, 0, 0))]
        + [vmem] * 5,
        out_specs=vmem,
        scratch_shapes=[
            pltpu.VMEM((3 * rows + 1, 8, 128), F32),
            pltpu.VMEM((steps * chunk, 8, 128), F32),
            pltpu.VMEM((rows - 1, 1024), F32),
            pltpu.VMEM((top_rows, 1024), F32),
            pltpu.VMEM((16 * slots, 1024), F32),
            pltpu.VMEM((128, 1024), F32),
            pltpu.VMEM((2 * branches - 1, 8, 128), F32),
            pltpu.VMEM((128, 1024), BF16),
            pltpu.VMEM((1024, 128), BF16),
        ],
        compiler_params=pltpu.CompilerParams(vmem_limit_bytes=VMEM_BYTES),
        cost_estimate=pl.CostEstimate(flops=10**9, bytes_accessed=16 << 20, transcendentals=0),
        name="far",
    )


def on_device(
    points,
    charges,
    leaf_basis,
    low_transfer,
    low_coupling,
    low_partner,
    top_transfer,
    top_coupling,
    top_partner,
    near_list,
):
    branches = lax.axis_size("branch")
    me = lax.axis_index("branch")
    leaves = leaf_basis.shape[0]
    rows = 2 * leaves - 1
    reach = leaves // 4
    up = [(i, i + 1) for i in range(branches - 1)]
    down = [(i + 1, i) for i in range(branches - 1)]
    length, width = points.shape[1], reach * leaf_basis.shape[2]
    pts_before = lax.ppermute(points[:, length - width :], "branch", up)
    pts_after = lax.ppermute(points[:, :width], "branch", down)
    chg_before = lax.ppermute(charges[:, length - width :], "branch", up)
    chg_after = lax.ppermute(charges[:, :width], "branch", down)
    basis = leaf_basis.reshape(leaves * 32, 128)
    coef, last, first = make_upward(leaves)(charges, basis, low_transfer)
    before = lax.ppermute(last, "branch", up)
    after = lax.ppermute(first, "branch", down)
    roots = lax.all_gather(coef[rows - 1 :], "branch", axis=0, tiled=True)
    near_rows = jnp.where(near_list >= 0, near_list - (me * leaves - reach), leaves + 2 * reach)
    near = make_near(leaves, near_list.shape[1])(
        near_rows.reshape(-1), points, pts_before, pts_after, charges, chg_before, chg_after
    )
    partner_rows = jnp.where(low_partner >= 0, low_partner - (me - 1) * rows, 3 * rows)
    return make_far(leaves, branches, low_partner.shape[1], top_partner.shape[1])(
        me.reshape(1),
        partner_rows.reshape(-1),
        top_partner.reshape(-1),
        coef,
        before,
        after,
        roots,
        low_coupling,
        low_transfer,
        top_transfer,
        top_coupling,
        basis,
        near,
    )


def solution(mesh):
    return jax.shard_map(
        on_device,
        mesh=mesh,
        in_specs=(
            P(None, "branch"),
            P(None, "branch"),
            P("branch", None, None),
            P("branch", None),
            P("branch", None, None),
            P("branch", None),
            P(),
            P(),
            P(),
            P("branch", None),
        ),
        out_specs=P(None, "branch"),
        check_vma=False,
    )
```

```python
import math

import jax
import jax.numpy as jnp
from jax import lax
from jax.experimental import pallas as pl
from jax.experimental.pallas import tpu as pltpu
from jax.sharding import PartitionSpec as P

SOFTEN = 0.0025
FOURPI = 4.0 * math.pi
F32 = jnp.float32
BF16 = jnp.bfloat16
VMEM_BYTES = 60 << 20
GROUP = 32


def level_start(total, depth_at):
    return 2 * total - (2 * total >> depth_at)


def halo_counts(leaves, depth):
    return [max(1, (leaves // 4) >> k) for k in range(depth + 1)]


def lane_group(shape):
    return lax.broadcasted_iota(jnp.int32, shape, len(shape) - 1) // 32


def spread_groups(z):
    z = z + pltpu.roll(z, 32, axis=z.ndim - 1)
    return z + pltpu.roll(z, 64, axis=z.ndim - 1)


def expand_matrix():
    r = lax.broadcasted_iota(jnp.int32, (128, 1024), 0)
    c = lax.broadcasted_iota(jnp.int32, (128, 1024), 1)
    return jnp.where(((r % 32) == (c // 32)) & (r < 96), 1.0, 0.0).astype(BF16)


def reduce_matrix():
    r = lax.broadcasted_iota(jnp.int32, (1024, 128), 0)
    c = lax.broadcasted_iota(jnp.int32, (1024, 128), 1)
    return jnp.where((r // 32) == (c % 32), 1.0, 0.0).astype(BF16)


def expand(u, xmat):
    hi = u.astype(BF16).astype(F32)
    rest = u - hi
    mid = rest.astype(BF16).astype(F32)
    low = rest - mid
    group = lane_group(u.shape)
    parts = jnp.where(group == 0, hi, jnp.where(group == 1, mid, jnp.where(group == 2, low, 0.0)))
    return jnp.dot(parts.astype(BF16), xmat, preferred_element_type=F32)


def reduce32(acc, rmat):
    hi = acc.astype(BF16)
    low = (acc - hi.astype(F32)).astype(BF16)
    return jnp.dot(hi, rmat, preferred_element_type=F32) + jnp.dot(
        low, rmat, preferred_element_type=F32
    )


def point_rows(points):
    n = points.shape[1]
    row = lax.broadcasted_iota(jnp.int32, (8, n), 0)
    scaled = (points - 0.5) * FOURPI
    value = jnp.where(
        row == 0, scaled[0:1], jnp.where(row == 1, scaled[1:2], jnp.where(row == 2, scaled[2:3], 0.0))
    )
    high = value.astype(BF16).astype(F32)
    low = (value - high).astype(BF16).astype(F32)
    both = high + low
    norm = jnp.sum(both * both, axis=0, keepdims=True)
    return row, high, low, norm


def three_parts(norm):
    one = norm.astype(BF16).astype(F32)
    rest = norm - one
    two = rest.astype(BF16).astype(F32)
    return one, two, rest - two


def source_rows(row, high, low, norm):
    m1, m2, m3 = three_parts(norm)
    unit = row == 4
    s0 = jnp.where(row == 3, m1, jnp.where(unit, 1.0, high))
    s1 = jnp.where(row == 3, m2, jnp.where(unit, 1.0, low))
    s2 = jnp.where(row == 3, m3, jnp.where(unit, 1.0, high))
    return jnp.concatenate([s0, s1, s2, low], axis=0).astype(BF16)


def target_rows(row, high, low, norm):
    n1, n2, n3 = three_parts(norm + SOFTEN * FOURPI * FOURPI)
    unit = row == 3
    t0 = jnp.where(row == 4, n1, jnp.where(unit, 1.0, -2.0 * high))
    t1 = jnp.where(row == 4, n2, jnp.where(unit, 1.0, -2.0 * high))
    t2 = jnp.where(row == 4, n3, jnp.where(unit, 1.0, -2.0 * low))
    return jnp.concatenate([t0, t1, t2, -2.0 * low], axis=0).astype(BF16)


def spread_row(ref, at):
    return ref[pl.ds(at, 8, stride=0), :]


def move_up(u_ref, e_ref, xmat_ref, src, dst, e_row, width):
    group = min(GROUP, width)

    def step(i, carry):
        first = i * group
        mats = e_ref.at[pl.ds(pl.multiple_of(e_row + first, 8), group)] if group >= 8 else e_ref
        skip = 0 if group >= 8 else e_row
        u = u_ref[pl.ds(src + first, group)].reshape(group * 8, 128)
        wide = expand(u, xmat_ref[...])
        for n in range(0, group, 2):
            total = None
            for m in (n, n + 1):
                prod = wide[8 * m : 8 * m + 8] * spread_row(mats, skip + m)
                for j in range(8):
                    piece = prod[:, 128 * j : 128 * j + 128]
                    total = piece if total is None else total + piece
            u_ref[dst + i * (group // 2) + n // 2] = spread_groups(total)
        return carry

    if width == group:
        step(0, 0)
    else:
        lax.fori_loop(0, width // group, step, 0)


def upcast_rows(dst_ref, src_ref, rows):
    for first in range(0, rows, 64):
        count = min(64, rows - first)
        dst_ref[first : first + count, :] = src_ref[first : first + count, :].astype(F32)


def rounds_of(branches):
    rounds, stride = [], 1
    while stride < branches:
        size = 2 if stride == 1 or branches // stride == 2 else 4
        rounds.append((size, stride))
        stride *= size
    return rounds


def make_product(leaves, branches, near_slots, slots, top_slots):
    depth = leaves.bit_length() - 1
    depth_top = branches.bit_length() - 1
    counts = halo_counts(leaves, depth)
    packs = -(-sum(counts) // 4)
    rows = 2 * leaves - 1
    own = rows
    reach = leaves // 4
    span = leaves + 2 * reach
    edge = reach * 128
    length = leaves * 128
    unroll = 4
    wide = near_slots * 128
    top_rows = 2 * branches - 4
    rounds = rounds_of(branches)
    n_round = sum(size - 1 for size, _ in rounds)
    loop_steps = leaves // (2 * unroll)

    def kernel(
        index_ref,
        partner_ref,
        top_partner_ref,
        pts_ref,
        chg_ref,
        basis_hbm,
        transfer_hbm,
        coupling_hbm,
        top_transfer_hbm,
        top_coupling_hbm,
        out_ref,
        basis_ref,
        transfer_ref,
        coupling_ref,
        top_transfer_ref,
        top_coupling_ref,
        pts_before_ref,
        pts_after_ref,
        chg_before_ref,
        chg_after_ref,
        last_ref,
        first_ref,
        before_ref,
        after_ref,
        table_ref,
        upper_ref,
        far_ref,
        e_ref,
        top_e_ref,
        src_ref,
        tgt_ref,
        load_ref,
        tile_ref,
        rhs_ref,
        c_ref,
        acc_ref,
        xmat_ref,
        rmat_ref,
        load_sem,
        send_sem,
        recv_sem,
    ):
        me = lax.axis_index("branch")
        fetches = [
            pltpu.make_async_copy(a, b, load_sem.at[i])
            for i, (a, b) in enumerate(
                (
                    (basis_hbm, basis_ref),
                    (transfer_hbm, transfer_ref),
                    (coupling_hbm, coupling_ref.at[0:rows]),
                    (top_transfer_hbm, top_transfer_ref),
                    (top_coupling_hbm, top_coupling_ref),
                )
            )
        ]
        for fetch in fetches:
            fetch.start()

        right = (me + 1) % branches
        left = (me + branches - 1) % branches
        peers = []
        for size, stride in rounds:
            digit = (me // stride) % size
            for t in range(1, size):
                peers.append(me + ((digit + t) % size - digit) * stride)
        barrier = pltpu.get_barrier_semaphore()
        for other in [left, right] + peers:
            pl.semaphore_signal(
                barrier, inc=1, device_id=(other,), device_id_type=pl.DeviceIdType.MESH
            )

        def remote(i, a, b, other):
            return pltpu.make_async_remote_copy(
                src_ref=a,
                dst_ref=b,
                send_sem=send_sem.at[i],
                recv_sem=recv_sem.at[i],
                device_id=(other,),
                device_id_type=pl.DeviceIdType.MESH,
            )

        halos = [
            remote(0, pts_ref.at[:, length - edge : length], pts_before_ref, right),
            remote(1, chg_ref.at[:, length - edge : length], chg_before_ref, right),
            remote(2, pts_ref.at[:, 0:edge], pts_after_ref, left),
            remote(3, chg_ref.at[:, 0:edge], chg_after_ref, left),
        ]
        coef_halos = [
            remote(4, last_ref, before_ref, right),
            remote(5, first_ref, after_ref, left),
        ]
        gathers, at = [], 0
        for size, stride in rounds:
            block = pl.ds((me // stride) * stride, stride)
            gathers.append(
                [
                    remote(6 + at + t, upper_ref.at[block], upper_ref.at[block], peers[at + t])
                    for t in range(size - 1)
                ]
            )
            at += size - 1

        xmat_ref[...] = expand_matrix()
        rmat_ref[...] = reduce_matrix()

        fetches[0].wait()

        def leaf_up(i, carry):
            at = pl.multiple_of(i * 1024, 1024)
            loads = chg_ref[:, pl.ds(at, 1024)]
            loads = jnp.concatenate([loads[:, 128 * g : 128 * g + 128] for g in range(8)], axis=0)
            basis = basis_ref[pl.ds(pl.multiple_of(i * 256, 256), 256), :]
            out = lax.dot_general(
                loads.astype(BF16), basis, (((1,), (1,)), ((), ())), preferred_element_type=F32
            )
            group = lane_group((8, 128))
            for g in range(8):
                piece = out[8 * g : 8 * g + 8, 128 * (g // 4) : 128 * (g // 4) + 128]
                table_ref[own + i * 8 + g] = spread_groups(jnp.where(group == g % 4, piece, 0.0))
            return carry

        lax.fori_loop(0, leaves // 8, leaf_up, 0, unroll=4)

        pl.semaphore_wait(barrier, 2 + len(peers))
        for copy in halos:
            copy.start()

        fetches[1].wait()
        upcast_rows(e_ref, transfer_ref, rows - 1)
        for k in range(depth):
            start = level_start(leaves, k)
            move_up(
                table_ref,
                e_ref,
                xmat_ref,
                own + start,
                own + level_start(leaves, k + 1),
                start,
                leaves >> k,
            )

        lane = lane_group((8, 128))
        for pack_ref, tail in ((last_ref, True), (first_ref, False)):
            nodes = []
            for k in range(depth + 1):
                start, width = level_start(leaves, k), leaves >> k
                begin = start + width - counts[k] if tail else start
                nodes += list(range(begin, begin + counts[k]))
            for at in range(0, len(nodes), 4):
                four = nodes[at : at + 4]
                packed = table_ref[own + four[0]]
                for g in range(1, len(four)):
                    packed = jnp.where(lane == g, table_ref[own + four[g]], packed)
                pack_ref[at // 4] = packed
        for copy in coef_halos:
            copy.start()
        upper_ref[pl.ds(me, 1)] = table_ref[own + rows - 1 : own + rows]
        for copy in gathers[0]:
            copy.start()

        def prepare(points, charges, first, is_own, count):
            def step(i, carry):
                at = pl.multiple_of(i * 1024, 1024)
                parts = point_rows(points[:, pl.ds(at, 1024)])
                source = source_rows(*parts)
                loads = charges[:, pl.ds(at, 1024)]
                for g in range(8):
                    src_ref[first + i * 8 + g] = source[:, 128 * g : 128 * g + 128]
                    load_ref[first + i * 8 + g] = loads[:, 128 * g : 128 * g + 128]
                if is_own:
                    target = target_rows(*parts)
                    for g in range(8):
                        tgt_ref[i * 8 + g] = target[:, 128 * g : 128 * g + 128]
                return carry

            lax.fori_loop(0, count // 8, step, 0)

        prepare(pts_ref, chg_ref, reach, True, leaves)
        for copy in halos:
            copy.wait_recv()
        prepare(pts_before_ref, chg_before_ref, 0, False, reach)
        prepare(pts_after_ref, chg_after_ref, reach + leaves, False, reach)
        src_ref[span] = src_ref[reach]
        load_ref[span] = jnp.zeros((8, 128), F32)

        def tiles_of(leaf, slot, j):
            target = tgt_ref[leaf]
            for s in range(near_slots):
                q = index_ref[leaf * near_slots + s]
                square = lax.dot_general(
                    src_ref[q], target, (((0,), (0,)), ((), ())), preferred_element_type=F32
                )
                tile_ref[slot, j, 128 * s : 128 * s + 128, :] = lax.rsqrt(square).astype(BF16)
                rhs_ref[slot, j, :, 128 * s : 128 * s + 128] = load_ref[q]

        def apply(leaf, slot, j):
            at = pl.multiple_of(leaf * 128, 128)
            out_ref[:, pl.ds(at, 128)] = jnp.dot(
                rhs_ref[slot, j].astype(BF16), tile_ref[slot, j], preferred_element_type=F32
            )

        for j in range(unroll):
            tiles_of(j, 0, j)

        def near_step(i, carry):
            for half in range(2):
                base = (2 * i + half) * unroll
                for j in range(unroll):
                    tiles_of((base + unroll + j) % leaves, 1 - half, j)
                for j in range(unroll):
                    apply(base + j, half, j)
            for r in range(1, len(rounds)):

                @pl.when(i == (r * loop_steps) // (len(rounds) + 1))
                def _():
                    for copy in gathers[r - 1]:
                        copy.wait_recv()
                    for copy in gathers[r]:
                        copy.start()

            return carry

        lax.fori_loop(0, loop_steps, near_step, 0)

        table_ref[3 * rows] = jnp.zeros((8, 128), F32)
        for copy in coef_halos:
            copy.wait_recv()
        for in_ref, tail, base in ((before_ref, True, 0), (after_ref, False, 2 * rows)):
            at = 0
            for k in range(depth + 1):
                start, width = level_start(leaves, k), leaves >> k
                begin = base + (start + width - counts[k] if tail else start)
                for i in range(counts[k]):
                    packed = in_ref[(at + i) // 4]
                    table_ref[begin + i] = spread_groups(
                        jnp.where(lane == (at + i) % 4, packed, 0.0)
                    )
                at += counts[k]

        coupling_ref[rows] = jnp.zeros((slots, 1024), BF16)
        fetches[2].wait()

        def couple(i, carry):
            first = i * 16
            c_ref[...] = coupling_ref[pl.ds(first, 16)].reshape(16 * slots, 1024).astype(F32)
            for n in range(16):
                acc = [None] * 8
                for s in range(slots):
                    u = table_ref[partner_ref[(first + n) * slots + s]]
                    row = spread_row(c_ref, n * slots + s)
                    for j in range(8):
                        piece = u * row[:, 128 * j : 128 * j + 128]
                        acc[j] = piece if acc[j] is None else acc[j] + piece
                for j in range(8):
                    acc_ref[8 * n : 8 * n + 8, 128 * j : 128 * j + 128] = acc[j]
            far = reduce32(acc_ref[0:128], rmat_ref[...])
            far_ref[pl.ds(first, 16)] = far.reshape(16, 8, 128)
            return carry

        lax.fori_loop(0, 2 * leaves // 16, couple, 0)

        fetches[3].wait()
        fetches[4].wait()
        upcast_rows(top_e_ref, top_transfer_ref, top_rows)
        for copy in gathers[-1]:
            copy.wait_recv()
        for u in range(depth_top - 1):
            src = level_start(branches, u)
            move_up(
                upper_ref, top_e_ref, xmat_ref, src, level_start(branches, u + 1), src, branches >> u
            )
        upper_ref[2 * branches - 2] = jnp.zeros((8, 128), F32)
        for u in range(1, depth_top):
            row_at = level_start(branches, u) - branches + me // (1 << u)
            mats = top_coupling_ref[row_at].astype(F32)
            acc = [None] * 8
            for s in range(top_slots):
                entry = top_partner_ref[row_at * top_slots + s]
                at = jnp.where(entry >= 0, level_start(branches, u) + entry, 2 * branches - 2)
                value = upper_ref[at]
                for j in range(8):
                    piece = value * mats[s : s + 1, 128 * j : 128 * j + 128]
                    acc[j] = piece if acc[j] is None else acc[j] + piece
            for j in range(8):
                acc_ref[8 * u - 8 : 8 * u, 128 * j : 128 * j + 128] = acc[j]
        far_top = reduce32(acc_ref[0 : 8 * (depth_top - 1)], rmat_ref[...])

        def down(value, row):
            return reduce32(jnp.concatenate([value] * 8, axis=1) * row, rmat_ref[...])

        current = far_top[8 * (depth_top - 2) :]
        for u in range(depth_top - 2, 0, -1):
            row = top_e_ref[pl.ds(level_start(branches, u) + me // (1 << u), 1), :]
            current = far_top[8 * u - 8 : 8 * u] + down(current, row)
        far_ref[rows - 1] = far_ref[rows - 1] + down(current, top_e_ref[pl.ds(me, 1), :])

        for k in range(depth - 1, -1, -1):
            start, width = level_start(leaves, k), leaves >> k
            parents = level_start(leaves, k + 1)
            size = min(GROUP, width)

            def level(i, carry, start=start, parents=parents, size=size):
                at = pl.multiple_of(start + i * size, 8) if size >= 8 else 0
                mats = e_ref.at[pl.ds(at, size)] if size >= 8 else e_ref
                skip = 0 if size >= 8 else start
                for n in range(size):
                    value = far_ref[parents + i * (size // 2) + n // 2]
                    row = spread_row(mats, skip + n)
                    for j in range(8):
                        acc_ref[8 * n : 8 * n + 8, 128 * j : 128 * j + 128] = (
                            value * row[:, 128 * j : 128 * j + 128]
                        )
                moved = reduce32(acc_ref[0 : 8 * size], rmat_ref[...])
                at = pl.ds(start + i * size, size)
                far_ref[at] = far_ref[at] + moved.reshape(size, 8, 128)
                return carry

            if width == size:
                level(0, 0)
            else:
                lax.fori_loop(0, width // size, level, 0)

        def leaf_down(i, carry):
            pieces = []
            for g in range(8):
                only = jnp.where(lane == g % 4, far_ref[i * 8 + g], 0.0)
                none = jnp.zeros((8, 128), F32)
                pieces.append(jnp.concatenate([only, none] if g < 4 else [none, only], axis=1))
            coefs = jnp.concatenate(pieces, axis=0).astype(BF16)
            basis = basis_ref[pl.ds(pl.multiple_of(i * 256, 256), 256), :]
            values = jnp.dot(coefs, basis, preferred_element_type=F32)
            for g in range(8):
                at = pl.ds(pl.multiple_of((i * 8 + g) * 128, 128), 128)
                out_ref[:, at] = out_ref[:, at] + values[8 * g : 8 * g + 8]
            return carry

        lax.fori_loop(0, leaves // 8, leaf_down, 0, unroll=4)
        for copy in halos + coef_halos + [copy for group in gathers for copy in group]:
            copy.wait_send()

    smem = pl.BlockSpec(memory_space=pltpu.SMEM)
    vmem = pl.BlockSpec(memory_space=pltpu.VMEM)
    hbm = pl.BlockSpec(memory_space=pl.ANY)
    n_copies = 6 + n_round
    return pl.pallas_call(
        kernel,
        out_shape=jax.ShapeDtypeStruct((8, length), F32),
        in_specs=[smem] * 3 + [vmem] * 2 + [hbm] * 5,
        out_specs=vmem,
        scratch_shapes=[
            pltpu.VMEM((leaves * 32, 128), BF16),
            pltpu.VMEM((rows - 1, 1024), BF16),
            pltpu.VMEM((rows + 1, slots, 1024), BF16),
            pltpu.VMEM((top_rows, 1024), BF16),
            pltpu.VMEM((branches - 2, top_slots, 1024), BF16),
            pltpu.VMEM((3, edge), F32),
            pltpu.VMEM((3, edge), F32),
            pltpu.VMEM((8, edge), F32),
            pltpu.VMEM((8, edge), F32),
            pltpu.VMEM((packs, 8, 128), F32),
            pltpu.VMEM((packs, 8, 128), F32),
            pltpu.VMEM((packs, 8, 128), F32),
            pltpu.VMEM((packs, 8, 128), F32),
            pltpu.VMEM((3 * rows + 1, 8, 128), F32),
            pltpu.VMEM((2 * branches - 1, 8, 128), F32),
            pltpu.VMEM((rows + 1, 8, 128), F32),
            pltpu.VMEM((rows - 1, 1024), F32),
            pltpu.VMEM((top_rows, 1024), F32),
            pltpu.VMEM((span + 1, 32, 128), BF16),
            pltpu.VMEM((leaves, 32, 128), BF16),
            pltpu.VMEM((span + 1, 8, 128), F32),
            pltpu.VMEM((2, unroll, wide, 128), BF16),
            pltpu.VMEM((2, unroll, 8, wide), F32),
            pltpu.VMEM((16 * slots, 1024), F32),
            pltpu.VMEM((8 * GROUP, 1024), F32),
            pltpu.VMEM((128, 1024), BF16),
            pltpu.VMEM((1024, 128), BF16),
            pltpu.SemaphoreType.DMA((5,)),
            pltpu.SemaphoreType.DMA((n_copies,)),
            pltpu.SemaphoreType.DMA((n_copies,)),
        ],
        compiler_params=pltpu.CompilerParams(
            vmem_limit_bytes=VMEM_BYTES, collective_id=0, has_side_effects=True
        ),
        cost_estimate=pl.CostEstimate(
            flops=4 * 10**10,
            bytes_accessed=16 << 20,
            transcendentals=leaves * near_slots * 128 * 128,
        ),
        name="product",
    )


def on_device(
    points,
    charges,
    leaf_basis,
    low_transfer,
    low_coupling,
    low_partner,
    top_transfer,
    top_coupling,
    top_partner,
    near_list,
):
    branches = lax.axis_size("branch")
    me = lax.axis_index("branch")
    leaves = leaf_basis.shape[0]
    rows = 2 * leaves - 1
    reach = leaves // 4
    near_rows = jnp.where(near_list >= 0, near_list - (me * leaves - reach), leaves + 2 * reach)
    partner_rows = jnp.where(low_partner >= 0, low_partner - (me - 1) * rows, 3 * rows)
    partner_rows = jnp.pad(partner_rows, ((0, 1), (0, 0)), constant_values=3 * rows)
    return make_product(
        leaves, branches, near_list.shape[1], low_partner.shape[1], top_partner.shape[1]
    )(
        near_rows.reshape(-1),
        partner_rows.reshape(-1),
        top_partner.reshape(-1),
        points,
        charges,
        leaf_basis.reshape(leaves * 32, 128),
        low_transfer,
        low_coupling,
        top_transfer,
        top_coupling,
    )


def solution(mesh):
    return jax.shard_map(
        on_device,
        mesh=mesh,
        in_specs=(
            P(None, "branch"),
            P(None, "branch"),
            P("branch", None, None),
            P("branch", None),
            P("branch", None, None),
            P("branch", None),
            P(),
            P(),
            P(),
            P("branch", None),
        ),
        out_specs=P(None, "branch"),
        check_vma=False,
    )
```

```python
import math

import jax
import jax.numpy as jnp
from jax import lax
from jax.experimental import pallas as pl
from jax.experimental.pallas import tpu as pltpu
from jax.sharding import PartitionSpec as P

SOFTEN = 0.0025
FOURPI = 4.0 * math.pi
F32 = jnp.float32
BF16 = jnp.bfloat16
VMEM_BYTES = 60 << 20
GROUP = 32


def level_start(total, depth_at):
    return 2 * total - (2 * total >> depth_at)


def halo_counts(leaves, depth):
    return [max(1, (leaves // 4) >> k) for k in range(depth + 1)]


def lane_group(shape):
    return lax.broadcasted_iota(jnp.int32, shape, len(shape) - 1) // 32


def spread_groups(z):
    z = z + pltpu.roll(z, 32, axis=z.ndim - 1)
    return z + pltpu.roll(z, 64, axis=z.ndim - 1)


def expand_matrix():
    r = lax.broadcasted_iota(jnp.int32, (128, 1024), 0)
    c = lax.broadcasted_iota(jnp.int32, (128, 1024), 1)
    return jnp.where(((r % 32) == (c // 32)) & (r < 96), 1.0, 0.0).astype(BF16)


def reduce_matrix():
    r = lax.broadcasted_iota(jnp.int32, (1024, 128), 0)
    c = lax.broadcasted_iota(jnp.int32, (1024, 128), 1)
    return jnp.where((r // 32) == (c % 32), 1.0, 0.0).astype(BF16)


def expand(u, xmat):
    hi = u.astype(BF16).astype(F32)
    rest = u - hi
    mid = rest.astype(BF16).astype(F32)
    low = rest - mid
    group = lane_group(u.shape)
    parts = jnp.where(group == 0, hi, jnp.where(group == 1, mid, jnp.where(group == 2, low, 0.0)))
    return jnp.dot(parts.astype(BF16), xmat, preferred_element_type=F32)


def reduce32(acc, rmat):
    hi = acc.astype(BF16)
    low = (acc - hi.astype(F32)).astype(BF16)
    return jnp.dot(hi, rmat, preferred_element_type=F32) + jnp.dot(
        low, rmat, preferred_element_type=F32
    )


def point_rows(points):
    n = points.shape[1]
    row = lax.broadcasted_iota(jnp.int32, (8, n), 0)
    scaled = (points - 0.5) * FOURPI
    value = jnp.where(
        row == 0, scaled[0:1], jnp.where(row == 1, scaled[1:2], jnp.where(row == 2, scaled[2:3], 0.0))
    )
    high = value.astype(BF16).astype(F32)
    low = (value - high).astype(BF16).astype(F32)
    both = high + low
    norm = jnp.sum(both * both, axis=0, keepdims=True)
    return row, high, low, norm


def three_parts(norm):
    one = norm.astype(BF16).astype(F32)
    rest = norm - one
    two = rest.astype(BF16).astype(F32)
    return one, two, rest - two


def source_rows(row, high, low, norm):
    m1, m2, m3 = three_parts(norm)
    unit = row == 4
    s0 = jnp.where(row == 3, m1, jnp.where(unit, 1.0, high))
    s1 = jnp.where(row == 3, m2, jnp.where(unit, 1.0, low))
    s2 = jnp.where(row == 3, m3, jnp.where(unit, 1.0, high))
    return jnp.concatenate([s0, s1, s2, low], axis=0).astype(BF16)


def target_rows(row, high, low, norm):
    n1, n2, n3 = three_parts(norm + SOFTEN * FOURPI * FOURPI)
    unit = row == 3
    t0 = jnp.where(row == 4, n1, jnp.where(unit, 1.0, -2.0 * high))
    t1 = jnp.where(row == 4, n2, jnp.where(unit, 1.0, -2.0 * high))
    t2 = jnp.where(row == 4, n3, jnp.where(unit, 1.0, -2.0 * low))
    return jnp.concatenate([t0, t1, t2, -2.0 * low], axis=0).astype(BF16)


def spread_row(ref, at):
    return ref[pl.ds(at, 8, stride=0), :]


def move_up(u_ref, e_ref, xmat_ref, src, dst, e_row, width):
    group = min(GROUP, width)

    def step(i, carry):
        first = i * group
        mats = e_ref.at[pl.ds(pl.multiple_of(e_row + first, 8), group)] if group >= 8 else e_ref
        skip = 0 if group >= 8 else e_row
        u = u_ref[pl.ds(src + first, group)].reshape(group * 8, 128)
        wide = expand(u, xmat_ref[...])
        for n in range(0, group, 2):
            total = None
            for m in (n, n + 1):
                prod = wide[8 * m : 8 * m + 8] * spread_row(mats, skip + m)
                for j in range(8):
                    piece = prod[:, 128 * j : 128 * j + 128]
                    total = piece if total is None else total + piece
            u_ref[dst + i * (group // 2) + n // 2] = spread_groups(total)
        return carry

    if width == group:
        step(0, 0)
    else:
        lax.fori_loop(0, width // group, step, 0)


def upcast_rows(dst_ref, src_ref, rows):
    for first in range(0, rows, 64):
        count = min(64, rows - first)
        dst_ref[first : first + count, :] = src_ref[first : first + count, :].astype(F32)


def rounds_of(branches):
    rounds, stride = [], 1
    while stride < branches:
        size = 2 if stride == 1 or branches // stride == 2 else 4
        rounds.append((size, stride))
        stride *= size
    return rounds


def make_product(leaves, branches, near_slots, slots, top_slots):
    depth = leaves.bit_length() - 1
    depth_top = branches.bit_length() - 1
    counts = halo_counts(leaves, depth)
    packs = -(-sum(counts) // 4)
    rows = 2 * leaves - 1
    own = rows
    reach = leaves // 4
    span = leaves + 2 * reach
    edge = reach * 128
    length = leaves * 128
    unroll = 8
    chunk = 4 * unroll
    wide = near_slots * 128
    top_rows = 2 * branches - 4
    rounds = rounds_of(branches)
    n_round = sum(size - 1 for size, _ in rounds)
    loop_steps = leaves // (2 * unroll)

    def kernel(
        index_ref,
        partner_ref,
        top_partner_ref,
        pts_hbm,
        chg_hbm,
        basis_hbm,
        transfer_hbm,
        coupling_hbm,
        top_transfer_hbm,
        top_coupling_hbm,
        out_ref,
        pts_ref,
        chg_ref,
        basis_ref,
        transfer_ref,
        coupling_ref,
        top_transfer_ref,
        top_coupling_ref,
        pts_before_ref,
        pts_after_ref,
        chg_before_ref,
        chg_after_ref,
        last_ref,
        first_ref,
        before_ref,
        after_ref,
        table_ref,
        upper_ref,
        far_ref,
        e_ref,
        top_e_ref,
        src_ref,
        tgt_ref,
        load_ref,
        tile_ref,
        rhs_ref,
        c_ref,
        acc_ref,
        xmat_ref,
        rmat_ref,
        load_sem,
        send_sem,
        recv_sem,
    ):
        me = lax.axis_index("branch")
        fetches = [
            pltpu.make_async_copy(a, b, load_sem.at[i])
            for i, (a, b) in enumerate(
                (
                    (chg_hbm, chg_ref),
                    (basis_hbm, basis_ref),
                    (transfer_hbm, transfer_ref),
                    (coupling_hbm, coupling_ref.at[0:rows]),
                    (pts_hbm, pts_ref),
                    (top_transfer_hbm, top_transfer_ref),
                    (top_coupling_hbm, top_coupling_ref),
                )
            )
        ]
        for fetch in fetches:
            fetch.start()

        right = (me + 1) % branches
        left = (me + branches - 1) % branches
        peers = []
        for size, stride in rounds:
            digit = (me // stride) % size
            for t in range(1, size):
                peers.append(me + ((digit + t) % size - digit) * stride)
        barrier = pltpu.get_barrier_semaphore()
        for other in [left, right] + peers:
            pl.semaphore_signal(
                barrier, inc=1, device_id=(other,), device_id_type=pl.DeviceIdType.MESH
            )

        def remote(i, a, b, other):
            return pltpu.make_async_remote_copy(
                src_ref=a,
                dst_ref=b,
                send_sem=send_sem.at[i],
                recv_sem=recv_sem.at[i],
                device_id=(other,),
                device_id_type=pl.DeviceIdType.MESH,
            )

        halos = [
            remote(0, pts_hbm.at[:, length - edge : length], pts_before_ref, right),
            remote(1, chg_hbm.at[:, length - edge : length], chg_before_ref, right),
            remote(2, pts_hbm.at[:, 0:edge], pts_after_ref, left),
            remote(3, chg_hbm.at[:, 0:edge], chg_after_ref, left),
        ]
        coef_halos = [
            remote(4, last_ref, before_ref, right),
            remote(5, first_ref, after_ref, left),
        ]
        gathers, at = [], 0
        for size, stride in rounds:
            block = pl.ds((me // stride) * stride, stride)
            gathers.append(
                [
                    remote(6 + at + t, upper_ref.at[block], upper_ref.at[block], peers[at + t])
                    for t in range(size - 1)
                ]
            )
            at += size - 1

        xmat_ref[...] = expand_matrix()
        rmat_ref[...] = reduce_matrix()

        pl.semaphore_wait(barrier, 2 + len(peers))
        for copy in halos:
            copy.start()

        fetches[0].wait()
        fetches[1].wait()

        def leaf_up(i, carry):
            at = pl.multiple_of(i * 1024, 1024)
            loads = chg_ref[:, pl.ds(at, 1024)]
            loads = jnp.concatenate([loads[:, 128 * g : 128 * g + 128] for g in range(8)], axis=0)
            basis = basis_ref[pl.ds(pl.multiple_of(i * 256, 256), 256), :]
            out = lax.dot_general(
                loads.astype(BF16), basis, (((1,), (1,)), ((), ())), preferred_element_type=F32
            )
            group = lane_group((8, 128))
            for g in range(8):
                piece = out[8 * g : 8 * g + 8, 128 * (g // 4) : 128 * (g // 4) + 128]
                table_ref[own + i * 8 + g] = spread_groups(jnp.where(group == g % 4, piece, 0.0))
            return carry

        lax.fori_loop(0, leaves // 8, leaf_up, 0, unroll=4)

        fetches[2].wait()
        upcast_rows(e_ref, transfer_ref, rows - 1)
        for k in range(depth):
            start = level_start(leaves, k)
            move_up(
                table_ref,
                e_ref,
                xmat_ref,
                own + start,
                own + level_start(leaves, k + 1),
                start,
                leaves >> k,
            )

        lane = lane_group((8, 128))
        for pack_ref, tail in ((last_ref, True), (first_ref, False)):
            nodes = []
            for k in range(depth + 1):
                start, width = level_start(leaves, k), leaves >> k
                begin = start + width - counts[k] if tail else start
                nodes += list(range(begin, begin + counts[k]))
            for at in range(0, len(nodes), 4):
                four = nodes[at : at + 4]
                packed = table_ref[own + four[0]]
                for g in range(1, len(four)):
                    packed = jnp.where(lane == g, table_ref[own + four[g]], packed)
                pack_ref[at // 4] = packed
        for copy in coef_halos:
            copy.start()
        upper_ref[pl.ds(me, 1)] = table_ref[own + rows - 1 : own + rows]
        for copy in gathers[0]:
            copy.start()

        def prepare(points, charges, first, is_own, count):
            def step(i, carry):
                at = pl.multiple_of(i * 1024, 1024)
                parts = point_rows(points[:, pl.ds(at, 1024)])
                source = source_rows(*parts)
                loads = charges[:, pl.ds(at, 1024)]
                for g in range(8):
                    src_ref[first + i * 8 + g] = source[:, 128 * g : 128 * g + 128]
                    load_ref[first + i * 8 + g] = loads[:, 128 * g : 128 * g + 128]
                if is_own:
                    target = target_rows(*parts)
                    for g in range(8):
                        tgt_ref[i * 8 + g] = target[:, 128 * g : 128 * g + 128]
                return carry

            lax.fori_loop(0, count // 8, step, 0)

        fetches[4].wait()
        prepare(pts_ref, chg_ref, reach, True, leaves)
        for copy in halos:
            copy.wait_recv()
        prepare(pts_before_ref, chg_before_ref, 0, False, reach)
        prepare(pts_after_ref, chg_after_ref, reach + leaves, False, reach)
        src_ref[span] = src_ref[reach]
        load_ref[span] = jnp.zeros((8, 128), F32)

        def tiles_of(leaf, slot, j):
            target = tgt_ref[leaf]
            for s in range(near_slots):
                entry = index_ref[s, leaf]
                q = jnp.where(entry >= 0, jnp.maximum(entry - me * leaves + reach, 0), span)
                square = lax.dot_general(
                    src_ref[q], target, (((0,), (0,)), ((), ())), preferred_element_type=F32
                )
                tile_ref[slot, j, 128 * s : 128 * s + 128, :] = lax.rsqrt(square).astype(BF16)
                rhs_ref[slot, j, :, 128 * s : 128 * s + 128] = load_ref[q]

        def apply(leaf, slot, j):
            at = pl.multiple_of(leaf * 128, 128)
            out_ref[:, pl.ds(at, 128)] = jnp.dot(
                rhs_ref[slot, j].astype(BF16), tile_ref[slot, j], preferred_element_type=F32
            )

        table_ref[3 * rows] = jnp.zeros((8, 128), F32)
        for copy in coef_halos:
            copy.wait_recv()
        for in_ref, tail, base in ((before_ref, True, 0), (after_ref, False, 2 * rows)):
            at = 0
            for k in range(depth + 1):
                start, width = level_start(leaves, k), leaves >> k
                begin = base + (start + width - counts[k] if tail else start)
                for i in range(counts[k]):
                    packed = in_ref[(at + i) // 4]
                    table_ref[begin + i] = spread_groups(
                        jnp.where(lane == (at + i) % 4, packed, 0.0)
                    )
                at += counts[k]

        coupling_ref[rows] = jnp.zeros((slots, 1024), BF16)
        fetches[3].wait()

        def couple(first, n):
            node = first + n
            if n == chunk - 1:
                node = node % rows
            acc = [None] * 8
            for s in range(slots):
                entry = partner_ref[s, node]
                at = jnp.maximum(entry - (me - 1) * rows, 0)
                u = table_ref[jnp.where(entry >= 0, at, 3 * rows)]
                row = spread_row(c_ref, n * slots + s)
                for j in range(8):
                    piece = u * row[:, 128 * j : 128 * j + 128]
                    acc[j] = piece if acc[j] is None else acc[j] + piece
            for j in range(8):
                acc_ref[8 * n : 8 * n + 8, 128 * j : 128 * j + 128] = acc[j]

        for j in range(unroll):
            tiles_of(j, 0, j)

        def near_step(i, carry):
            first = i * chunk
            c_ref[...] = coupling_ref[pl.ds(first, chunk)].reshape(chunk * slots, 1024).astype(F32)
            for half in range(2):
                base = (2 * i + half) * unroll
                for j in range(unroll):
                    tiles_of((base + unroll + j) % leaves, 1 - half, j)
                    for n in range(2):
                        couple(first, 2 * (half * unroll + j) + n)
                for j in range(unroll):
                    apply(base + j, half, j)
            far = jnp.dot(acc_ref[...].astype(BF16), rmat_ref[...], preferred_element_type=F32)
            far_ref[pl.ds(first, chunk)] = far.reshape(chunk, 8, 128)
            for r in range(1, len(rounds)):

                @pl.when(i == (r * loop_steps) // (len(rounds) + 1))
                def _():
                    for copy in gathers[r - 1]:
                        copy.wait_recv()
                    for copy in gathers[r]:
                        copy.start()

            return carry

        lax.fori_loop(0, loop_steps, near_step, 0)

        fetches[5].wait()
        fetches[6].wait()
        upcast_rows(top_e_ref, top_transfer_ref, top_rows)
        for copy in gathers[-1]:
            copy.wait_recv()
        for u in range(depth_top - 1):
            src = level_start(branches, u)
            move_up(
                upper_ref, top_e_ref, xmat_ref, src, level_start(branches, u + 1), src, branches >> u
            )
        upper_ref[2 * branches - 2] = jnp.zeros((8, 128), F32)
        for u in range(1, depth_top):
            row_at = level_start(branches, u) - branches + me // (1 << u)
            mats = top_coupling_ref[row_at].astype(F32)
            acc = [None] * 8
            for s in range(top_slots):
                entry = top_partner_ref[s, row_at]
                at = jnp.where(entry >= 0, level_start(branches, u) + entry, 2 * branches - 2)
                value = upper_ref[at]
                for j in range(8):
                    piece = value * mats[s : s + 1, 128 * j : 128 * j + 128]
                    acc[j] = piece if acc[j] is None else acc[j] + piece
            for j in range(8):
                acc_ref[8 * u - 8 : 8 * u, 128 * j : 128 * j + 128] = acc[j]
        far_top = reduce32(acc_ref[0 : 8 * (depth_top - 1)], rmat_ref[...])

        def down(value, row):
            return reduce32(jnp.concatenate([value] * 8, axis=1) * row, rmat_ref[...])

        current = far_top[8 * (depth_top - 2) :]
        for u in range(depth_top - 2, 0, -1):
            row = top_e_ref[pl.ds(level_start(branches, u) + me // (1 << u), 1), :]
            current = far_top[8 * u - 8 : 8 * u] + down(current, row)
        far_ref[rows - 1] = far_ref[rows - 1] + down(current, top_e_ref[pl.ds(me, 1), :])

        for k in range(depth - 1, -1, -1):
            start, width = level_start(leaves, k), leaves >> k
            parents = level_start(leaves, k + 1)
            size = min(GROUP, width)

            def level(i, carry, start=start, parents=parents, size=size):
                at = pl.multiple_of(start + i * size, 8) if size >= 8 else 0
                mats = e_ref.at[pl.ds(at, size)] if size >= 8 else e_ref
                skip = 0 if size >= 8 else start
                for n in range(size):
                    value = far_ref[parents + i * (size // 2) + n // 2]
                    row = spread_row(mats, skip + n)
                    for j in range(8):
                        acc_ref[8 * n : 8 * n + 8, 128 * j : 128 * j + 128] = (
                            value * row[:, 128 * j : 128 * j + 128]
                        )
                moved = reduce32(acc_ref[0 : 8 * size], rmat_ref[...])
                at = pl.ds(start + i * size, size)
                far_ref[at] = far_ref[at] + moved.reshape(size, 8, 128)
                return carry

            if width == size:
                level(0, 0)
            else:
                lax.fori_loop(0, width // size, level, 0)

        def leaf_down(i, carry):
            pieces = []
            for g in range(8):
                only = jnp.where(lane == g % 4, far_ref[i * 8 + g], 0.0)
                none = jnp.zeros((8, 128), F32)
                pieces.append(jnp.concatenate([only, none] if g < 4 else [none, only], axis=1))
            coefs = jnp.concatenate(pieces, axis=0).astype(BF16)
            basis = basis_ref[pl.ds(pl.multiple_of(i * 256, 256), 256), :]
            values = jnp.dot(coefs, basis, preferred_element_type=F32)
            for g in range(8):
                at = pl.ds(pl.multiple_of((i * 8 + g) * 128, 128), 128)
                out_ref[:, at] = out_ref[:, at] + values[8 * g : 8 * g + 8]
            return carry

        lax.fori_loop(0, leaves // 8, leaf_down, 0, unroll=4)
        for copy in halos + coef_halos + [copy for group in gathers for copy in group]:
            copy.wait_send()

    smem = pl.BlockSpec(memory_space=pltpu.SMEM)
    vmem = pl.BlockSpec(memory_space=pltpu.VMEM)
    hbm = pl.BlockSpec(memory_space=pl.ANY)
    n_copies = 6 + n_round
    return pl.pallas_call(
        kernel,
        out_shape=jax.ShapeDtypeStruct((8, length), F32),
        in_specs=[smem] * 3 + [hbm] * 7,
        out_specs=vmem,
        scratch_shapes=[
            pltpu.VMEM((3, length), F32),
            pltpu.VMEM((8, length), F32),
            pltpu.VMEM((leaves * 32, 128), BF16),
            pltpu.VMEM((rows - 1, 1024), BF16),
            pltpu.VMEM((rows + 1, slots, 1024), BF16),
            pltpu.VMEM((top_rows, 1024), BF16),
            pltpu.VMEM((branches - 2, top_slots, 1024), BF16),
            pltpu.VMEM((3, edge), F32),
            pltpu.VMEM((3, edge), F32),
            pltpu.VMEM((8, edge), F32),
            pltpu.VMEM((8, edge), F32),
            pltpu.VMEM((packs, 8, 128), F32),
            pltpu.VMEM((packs, 8, 128), F32),
            pltpu.VMEM((packs, 8, 128), F32),
            pltpu.VMEM((packs, 8, 128), F32),
            pltpu.VMEM((3 * rows + 1, 8, 128), F32),
            pltpu.VMEM((2 * branches - 1, 8, 128), F32),
            pltpu.VMEM((rows + 1, 8, 128), F32),
            pltpu.VMEM((rows - 1, 1024), F32),
            pltpu.VMEM((top_rows, 1024), F32),
            pltpu.VMEM((span + 1, 32, 128), BF16),
            pltpu.VMEM((leaves, 32, 128), BF16),
            pltpu.VMEM((span + 1, 8, 128), F32),
            pltpu.VMEM((2, unroll, wide, 128), BF16),
            pltpu.VMEM((2, unroll, 8, wide), F32),
            pltpu.VMEM((chunk * slots, 1024), F32),
            pltpu.VMEM((8 * chunk, 1024), F32),
            pltpu.VMEM((128, 1024), BF16),
            pltpu.VMEM((1024, 128), BF16),
            pltpu.SemaphoreType.DMA((7,)),
            pltpu.SemaphoreType.DMA((n_copies,)),
            pltpu.SemaphoreType.DMA((n_copies,)),
        ],
        compiler_params=pltpu.CompilerParams(
            vmem_limit_bytes=VMEM_BYTES, collective_id=0, has_side_effects=True
        ),
        cost_estimate=pl.CostEstimate(
            flops=4 * 10**10,
            bytes_accessed=16 << 20,
            transcendentals=leaves * near_slots * 128 * 128,
        ),
        name="product",
    )


def on_device(
    points,
    charges,
    leaf_basis,
    low_transfer,
    low_coupling,
    low_partner,
    top_transfer,
    top_coupling,
    top_partner,
    near_list,
):
    branches = lax.axis_size("branch")
    leaves = leaf_basis.shape[0]
    return make_product(
        leaves, branches, near_list.shape[1], low_partner.shape[1], top_partner.shape[1]
    )(
        near_list.T,
        low_partner.T,
        top_partner.T,
        points,
        charges,
        leaf_basis.reshape(leaves * 32, 128),
        low_transfer,
        low_coupling,
        top_transfer,
        top_coupling,
    )


def solution(mesh):
    return jax.shard_map(
        on_device,
        mesh=mesh,
        in_specs=(
            P(None, "branch"),
            P(None, "branch"),
            P("branch", None, None),
            P("branch", None),
            P("branch", None, None),
            P("branch", None),
            P(),
            P(),
            P(),
            P("branch", None),
        ),
        out_specs=P(None, "branch"),
        check_vma=False,
    )
```

```python
import math

import jax
import jax.numpy as jnp
from jax import lax
from jax.experimental import pallas as pl
from jax.experimental.pallas import tpu as pltpu
from jax.sharding import PartitionSpec as P

SOFTEN = 0.0025
FOURPI = 4.0 * math.pi
F32 = jnp.float32
BF16 = jnp.bfloat16
VMEM_BYTES = 60 << 20
GROUP = 128


def level_start(total, depth_at):
    return 2 * total - (2 * total >> depth_at)


def halo_counts(leaves, depth):
    return [max(1, (leaves // 4) >> k) for k in range(depth + 1)]


def lane_group(shape):
    return lax.broadcasted_iota(jnp.int32, shape, len(shape) - 1) // 32


def spread_groups(z):
    z = z + pltpu.roll(z, 32, axis=z.ndim - 1)
    return z + pltpu.roll(z, 64, axis=z.ndim - 1)


def expand_matrix():
    r = lax.broadcasted_iota(jnp.int32, (128, 1024), 0)
    c = lax.broadcasted_iota(jnp.int32, (128, 1024), 1)
    return jnp.where(((r % 32) == (c // 32)) & (r < 96), 1.0, 0.0).astype(BF16)


def reduce_matrix():
    r = lax.broadcasted_iota(jnp.int32, (1024, 128), 0)
    c = lax.broadcasted_iota(jnp.int32, (1024, 128), 1)
    return jnp.where((r // 32) == (c % 32), 1.0, 0.0).astype(BF16)


def expand(u, xmat):
    hi = u.astype(BF16).astype(F32)
    rest = u - hi
    mid = rest.astype(BF16).astype(F32)
    low = rest - mid
    group = lane_group(u.shape)
    parts = jnp.where(group == 0, hi, jnp.where(group == 1, mid, jnp.where(group == 2, low, 0.0)))
    return jnp.dot(parts.astype(BF16), xmat, preferred_element_type=F32)


def reduce32(acc, rmat):
    hi = acc.astype(BF16)
    low = (acc - hi.astype(F32)).astype(BF16)
    return jnp.dot(hi, rmat, preferred_element_type=F32) + jnp.dot(
        low, rmat, preferred_element_type=F32
    )


def point_rows(points):
    n = points.shape[1]
    row = lax.broadcasted_iota(jnp.int32, (8, n), 0)
    scaled = (points - 0.5) * FOURPI
    value = jnp.where(
        row == 0, scaled[0:1], jnp.where(row == 1, scaled[1:2], jnp.where(row == 2, scaled[2:3], 0.0))
    )
    high = value.astype(BF16).astype(F32)
    low = (value - high).astype(BF16).astype(F32)
    both = high + low
    norm = jnp.sum(both * both, axis=0, keepdims=True)
    return row, high, low, norm


def three_parts(norm):
    one = norm.astype(BF16).astype(F32)
    rest = norm - one
    two = rest.astype(BF16).astype(F32)
    return one, two, rest - two


def source_rows(row, high, low, norm):
    m1, m2, m3 = three_parts(norm)
    unit = row == 4
    s0 = jnp.where(row == 3, m1, jnp.where(unit, 1.0, high))
    s1 = jnp.where(row == 3, m2, jnp.where(unit, 1.0, low))
    s2 = jnp.where(row == 3, m3, jnp.where(unit, 1.0, high))
    return jnp.concatenate([s0, s1, s2, low], axis=0).astype(BF16)


def target_rows(row, high, low, norm):
    n1, n2, n3 = three_parts(norm + SOFTEN * FOURPI * FOURPI)
    unit = row == 3
    t0 = jnp.where(row == 4, n1, jnp.where(unit, 1.0, -2.0 * high))
    t1 = jnp.where(row == 4, n2, jnp.where(unit, 1.0, -2.0 * high))
    t2 = jnp.where(row == 4, n3, jnp.where(unit, 1.0, -2.0 * low))
    return jnp.concatenate([t0, t1, t2, -2.0 * low], axis=0).astype(BF16)


def spread_row(ref, at):
    return ref[pl.ds(at, 8, stride=0), :]


def move_up(u_ref, e_ref, xmat_ref, src, dst, e_row, width):
    group = min(GROUP, width)

    def step(i, carry):
        first = i * group
        mats = e_ref.at[pl.ds(pl.multiple_of(e_row + first, 8), group)] if group >= 8 else e_ref
        skip = 0 if group >= 8 else e_row
        u = u_ref[pl.ds(src + first, group)].reshape(group * 8, 128)
        wide = expand(u, xmat_ref[...])
        for n in range(0, group, 2):
            total = None
            for m in (n, n + 1):
                prod = wide[8 * m : 8 * m + 8] * spread_row(mats, skip + m)
                for j in range(8):
                    piece = prod[:, 128 * j : 128 * j + 128]
                    total = piece if total is None else total + piece
            u_ref[dst + i * (group // 2) + n // 2] = spread_groups(total)
        return carry

    if width == group:
        step(0, 0)
    else:
        lax.fori_loop(0, width // group, step, 0)


def upcast_rows(dst_ref, src_ref, rows):
    for first in range(0, rows, 64):
        count = min(64, rows - first)
        dst_ref[first : first + count, :] = src_ref[first : first + count, :].astype(F32)


def rounds_of(branches):
    rounds, stride = [], 1
    while stride < branches:
        size = 2 if stride == 1 or branches // stride == 2 else 4
        rounds.append((size, stride))
        stride *= size
    return rounds


def make_product(leaves, branches, near_slots, slots, top_slots):
    depth = leaves.bit_length() - 1
    depth_top = branches.bit_length() - 1
    counts = halo_counts(leaves, depth)
    packs = -(-sum(counts) // 4)
    rows = 2 * leaves - 1
    own = rows
    reach = leaves // 4
    span = leaves + 2 * reach
    edge = reach * 128
    length = leaves * 128
    unroll = 8
    chunk = 4 * unroll
    wide = near_slots * 128
    top_rows = 2 * branches - 4
    rounds = rounds_of(branches)
    n_round = sum(size - 1 for size, _ in rounds)
    loop_steps = leaves // (2 * unroll)
    held = [1]
    for r in range(1, len(rounds)):
        held.append(4 * held[-1] + sum(min(2, 3 - n) for n in (1, 2) if 2 * r + n - 1 < depth_top))

    def upper_row(level, node):
        r = level // 2
        bits = 1 if level % 2 == 0 else 0
        row = (4 * held[r - 1] if r else 0) + (node & 1 if bits else (2 if r else 0))
        block = node >> bits
        for i in range(r + 1, len(rounds)):
            row = row + (block & 3) * held[i - 1]
            block = block >> 2
        return row


    def kernel(
        near_list_ref,
        low_partner_ref,
        top_partner_ref,
        pts_hbm,
        chg_hbm,
        basis_hbm,
        transfer_hbm,
        coupling_hbm,
        top_transfer_hbm,
        top_coupling_hbm,
        out_ref,
        near_rows_ref,
        partner_rows_ref,
        index_ref,
        partner_ref,
        pts_ref,
        chg_ref,
        basis_ref,
        transfer_ref,
        coupling_ref,
        top_transfer_ref,
        top_coupling_ref,
        pts_before_ref,
        pts_after_ref,
        chg_before_ref,
        chg_after_ref,
        last_ref,
        first_ref,
        before_ref,
        after_ref,
        table_ref,
        upper_ref,
        roots_ref,
        far_ref,
        e_ref,
        top_e_ref,
        src_ref,
        tgt_ref,
        load_ref,
        tile_ref,
        rhs_ref,
        c_ref,
        acc_ref,
        xmat_ref,
        rmat_ref,
        load_sem,
        send_sem,
        recv_sem,
    ):
        me = lax.axis_index("branch")
        fetches = [
            pltpu.make_async_copy(a, b, load_sem.at[i])
            for i, (a, b) in enumerate(
                (
                    (chg_hbm, chg_ref),
                    (basis_hbm, basis_ref),
                    (transfer_hbm, transfer_ref),
                    (coupling_hbm, coupling_ref.at[0:rows]),
                    (pts_hbm, pts_ref),
                    (top_transfer_hbm, top_transfer_ref),
                    (top_coupling_hbm, top_coupling_ref),
                )
            )
        ]
        for fetch in fetches:
            fetch.start()

        right = (me + 1) % branches
        left = (me + branches - 1) % branches
        peers = []
        for size, stride in rounds:
            digit = (me // stride) % size
            for t in range(1, size):
                peers.append(me + ((digit + t) % size - digit) * stride)
        barrier = pltpu.get_barrier_semaphore()
        for other in [left, right] + peers:
            pl.semaphore_signal(
                barrier, inc=1, device_id=(other,), device_id_type=pl.DeviceIdType.MESH
            )

        def remote(i, a, b, other):
            return pltpu.make_async_remote_copy(
                src_ref=a,
                dst_ref=b,
                send_sem=send_sem.at[i],
                recv_sem=recv_sem.at[i],
                device_id=(other,),
                device_id_type=pl.DeviceIdType.MESH,
            )

        halos = [
            remote(0, pts_hbm.at[:, length - edge : length], pts_before_ref, right),
            remote(1, chg_hbm.at[:, length - edge : length], chg_before_ref, right),
            remote(2, pts_hbm.at[:, 0:edge], pts_after_ref, left),
            remote(3, chg_hbm.at[:, 0:edge], chg_after_ref, left),
        ]
        coef_halos = [
            remote(4, last_ref, before_ref, right),
            remote(5, first_ref, after_ref, left),
        ]
        digits = [(me // stride) % size for size, stride in rounds]
        gathers, at = [], 0
        for r, (size, stride) in enumerate(rounds):
            if r == 0:
                block = roots_ref.at[pl.ds(digits[0], 1)]
            else:
                first = sum(digits[i] * held[i - 1] for i in range(r, len(rounds)))
                block = upper_ref.at[pl.ds(first, held[r - 1])]
            gathers.append(
                [remote(6 + at + t, block, block, peers[at + t]) for t in range(size - 1)]
            )
            at += size - 1

        def lift(children, e_row):
            wide = expand(jnp.concatenate(children, axis=0), xmat_ref[...])
            parents = []
            for n in range(0, len(children), 2):
                total = None
                for m in (n, n + 1):
                    prod = wide[8 * m : 8 * m + 8] * top_e_ref[pl.ds(e_row + m, 1), :]
                    for j in range(8):
                        piece = prod[:, 128 * j : 128 * j + 128]
                        total = piece if total is None else total + piece
                parents.append(spread_groups(total))
            return parents

        def after_round(r):
            for copy in gathers[r]:
                copy.wait_recv()
            if r == 0:
                first = sum(digits[i] * held[i - 1] for i in range(1, len(rounds)))
                upper_ref[first] = lift([roots_ref[0], roots_ref[1]], (me // 2) * 2)[0]
                return
            size, stride = rounds[r]
            first = sum(digits[i] * held[i - 1] for i in range(r + 1, len(rounds)))
            block = me // (size * stride)
            level = 2 * r
            children = [upper_ref[first + n * held[r - 1] + held[r - 1] - 1] for n in range(4)]
            two = lift(children, level_start(branches, level - 1) + 4 * block)
            for n in range(2):
                upper_ref[first + 4 * held[r - 1] + n] = two[n]
            if level + 1 < depth_top:
                one = lift(two, level_start(branches, level) + 2 * block)
                upper_ref[first + 4 * held[r - 1] + 2] = one[0]


        entry = near_list_ref[...]
        near_rows_ref[...] = jnp.where(
            entry >= 0, jnp.maximum(entry - me * leaves + reach, 0), span
        )
        entry = low_partner_ref[...]
        partner_rows_ref[...] = jnp.full((slots, rows + 1), 3 * rows, jnp.int32)
        partner_rows_ref[:, 0:rows] = jnp.where(
            entry >= 0, jnp.maximum(entry - (me - 1) * rows, 0), 3 * rows
        )
        lists = [
            pltpu.make_async_copy(near_rows_ref, index_ref, load_sem.at[7]),
            pltpu.make_async_copy(partner_rows_ref, partner_ref, load_sem.at[8]),
        ]
        for copy in lists:
            copy.start()

        xmat_ref[...] = expand_matrix()
        rmat_ref[...] = reduce_matrix()

        pl.semaphore_wait(barrier, 2 + len(peers))
        for copy in halos:
            copy.start()

        fetches[0].wait()
        fetches[1].wait()

        def leaf_up(i, carry):
            at = pl.multiple_of(i * 1024, 1024)
            loads = chg_ref[:, pl.ds(at, 1024)]
            loads = jnp.concatenate([loads[:, 128 * g : 128 * g + 128] for g in range(8)], axis=0)
            basis = basis_ref[pl.ds(pl.multiple_of(i * 256, 256), 256), :]
            out = lax.dot_general(
                loads.astype(BF16), basis, (((1,), (1,)), ((), ())), preferred_element_type=F32
            )
            group = lane_group((8, 128))
            for g in range(8):
                piece = out[8 * g : 8 * g + 8, 128 * (g // 4) : 128 * (g // 4) + 128]
                table_ref[own + i * 8 + g] = spread_groups(jnp.where(group == g % 4, piece, 0.0))
            return carry

        lax.fori_loop(0, leaves // 8, leaf_up, 0, unroll=4)

        fetches[2].wait()
        upcast_rows(e_ref, transfer_ref, rows - 1)
        for k in range(depth):
            start = level_start(leaves, k)
            move_up(
                table_ref,
                e_ref,
                xmat_ref,
                own + start,
                own + level_start(leaves, k + 1),
                start,
                leaves >> k,
            )

        lane = lane_group((8, 128))
        for pack_ref, tail in ((last_ref, True), (first_ref, False)):
            nodes = []
            for k in range(depth + 1):
                start, width = level_start(leaves, k), leaves >> k
                begin = start + width - counts[k] if tail else start
                nodes += list(range(begin, begin + counts[k]))
            for at in range(0, len(nodes), 4):
                four = nodes[at : at + 4]
                packed = table_ref[own + four[0]]
                for g in range(1, len(four)):
                    packed = jnp.where(lane == g, table_ref[own + four[g]], packed)
                pack_ref[at // 4] = packed
        for copy in coef_halos:
            copy.start()
        roots_ref[pl.ds(digits[0], 1)] = table_ref[own + rows - 1 : own + rows]
        for copy in gathers[0]:
            copy.start()

        def prepare(points, charges, first, is_own, count):
            def step(i, carry):
                at = pl.multiple_of(i * 1024, 1024)
                parts = point_rows(points[:, pl.ds(at, 1024)])
                source = source_rows(*parts)
                loads = charges[:, pl.ds(at, 1024)]
                for g in range(8):
                    src_ref[first + i * 8 + g] = source[:, 128 * g : 128 * g + 128]
                    load_ref[first + i * 8 + g] = loads[:, 128 * g : 128 * g + 128]
                if is_own:
                    target = target_rows(*parts)
                    for g in range(8):
                        tgt_ref[i * 8 + g] = target[:, 128 * g : 128 * g + 128]
                return carry

            lax.fori_loop(0, count // 8, step, 0)

        fetches[4].wait()
        prepare(pts_ref, chg_ref, reach, True, leaves)
        for copy in halos:
            copy.wait_recv()
        prepare(pts_before_ref, chg_before_ref, 0, False, reach)
        prepare(pts_after_ref, chg_after_ref, reach + leaves, False, reach)
        src_ref[span] = src_ref[reach]
        load_ref[span] = jnp.zeros((8, 128), F32)

        def tiles_of(leaf, slot, j):
            target = tgt_ref[leaf]
            for s in range(near_slots):
                q = index_ref[s, leaf]
                square = lax.dot_general(
                    src_ref[q], target, (((0,), (0,)), ((), ())), preferred_element_type=F32
                )
                tile_ref[slot, j, 128 * s : 128 * s + 128, :] = lax.rsqrt(square).astype(BF16)
                rhs_ref[slot, j, :, 128 * s : 128 * s + 128] = load_ref[q]

        def apply(leaf, slot, j):
            at = pl.multiple_of(leaf * 128, 128)
            out_ref[:, pl.ds(at, 128)] = jnp.dot(
                rhs_ref[slot, j].astype(BF16), tile_ref[slot, j], preferred_element_type=F32
            )

        table_ref[3 * rows] = jnp.zeros((8, 128), F32)
        for copy in coef_halos:
            copy.wait_recv()
        for in_ref, tail, base in ((before_ref, True, 0), (after_ref, False, 2 * rows)):
            at = 0
            for k in range(depth + 1):
                start, width = level_start(leaves, k), leaves >> k
                begin = base + (start + width - counts[k] if tail else start)
                for i in range(counts[k]):
                    packed = in_ref[(at + i) // 4]
                    table_ref[begin + i] = spread_groups(
                        jnp.where(lane == (at + i) % 4, packed, 0.0)
                    )
                at += counts[k]

        coupling_ref[rows] = jnp.zeros((slots, 1024), BF16)
        fetches[3].wait()

        def couple(first, n):
            node = first + n
            acc = [None] * 8
            for s in range(slots):
                u = table_ref[partner_ref[s, node]]
                row = spread_row(c_ref, n * slots + s)
                for j in range(8):
                    piece = u * row[:, 128 * j : 128 * j + 128]
                    acc[j] = piece if acc[j] is None else acc[j] + piece
            for j in range(8):
                acc_ref[8 * n : 8 * n + 8, 128 * j : 128 * j + 128] = acc[j]

        fetches[5].wait()
        fetches[6].wait()
        upcast_rows(top_e_ref, top_transfer_ref, top_rows)
        for copy in lists:
            copy.wait()
        for j in range(unroll):
            tiles_of(j, 0, j)

        def near_step(i, carry):
            first = i * chunk
            c_ref[...] = coupling_ref[pl.ds(first, chunk)].reshape(chunk * slots, 1024).astype(F32)
            for half in range(2):
                base = (2 * i + half) * unroll
                for j in range(unroll):
                    tiles_of((base + unroll + j) % leaves, 1 - half, j)
                    for n in range(2):
                        couple(first, 2 * (half * unroll + j) + n)
                for j in range(unroll):
                    apply(base + j, half, j)
            far = jnp.dot(acc_ref[0 : 8 * chunk].astype(BF16), rmat_ref[...], preferred_element_type=F32)
            far_ref[pl.ds(first, chunk)] = far.reshape(chunk, 8, 128)
            for r in range(1, len(rounds)):

                @pl.when(i == (r * loop_steps) // (len(rounds) + 1))
                def _():
                    after_round(r - 1)
                    for copy in gathers[r]:
                        copy.start()

            return carry

        lax.fori_loop(0, loop_steps, near_step, 0)

        after_round(len(rounds) - 1)
        upper_ref[held[-1]] = jnp.zeros((8, 128), F32)
        for u in range(1, depth_top):
            row_at = level_start(branches, u) - branches + me // (1 << u)
            mats = top_coupling_ref[row_at].astype(F32)
            acc = [None] * 8
            for s in range(top_slots):
                entry = top_partner_ref[s, row_at]
                at = jnp.where(entry >= 0, upper_row(u, jnp.maximum(entry, 0)), held[-1])
                value = upper_ref[at]
                for j in range(8):
                    piece = value * mats[s : s + 1, 128 * j : 128 * j + 128]
                    acc[j] = piece if acc[j] is None else acc[j] + piece
            for j in range(8):
                acc_ref[8 * u - 8 : 8 * u, 128 * j : 128 * j + 128] = acc[j]
        far_top = reduce32(acc_ref[0 : 8 * (depth_top - 1)], rmat_ref[...])

        def down(value, row):
            return reduce32(jnp.concatenate([value] * 8, axis=1) * row, rmat_ref[...])

        current = far_top[8 * (depth_top - 2) :]
        for u in range(depth_top - 2, 0, -1):
            row = top_e_ref[pl.ds(level_start(branches, u) + me // (1 << u), 1), :]
            current = far_top[8 * u - 8 : 8 * u] + down(current, row)
        far_ref[rows - 1] = far_ref[rows - 1] + down(current, top_e_ref[pl.ds(me, 1), :])

        for k in range(depth - 1, -1, -1):
            start, width = level_start(leaves, k), leaves >> k
            parents = level_start(leaves, k + 1)
            size = min(GROUP, width)

            def level(i, carry, start=start, parents=parents, size=size):
                at = pl.multiple_of(start + i * size, 8) if size >= 8 else 0
                mats = e_ref.at[pl.ds(at, size)] if size >= 8 else e_ref
                skip = 0 if size >= 8 else start
                for n in range(size):
                    value = far_ref[parents + i * (size // 2) + n // 2]
                    row = spread_row(mats, skip + n)
                    for j in range(8):
                        acc_ref[8 * n : 8 * n + 8, 128 * j : 128 * j + 128] = (
                            value * row[:, 128 * j : 128 * j + 128]
                        )
                moved = reduce32(acc_ref[0 : 8 * size], rmat_ref[...])
                at = pl.ds(start + i * size, size)
                far_ref[at] = far_ref[at] + moved.reshape(size, 8, 128)
                return carry

            if width == size:
                level(0, 0)
            else:
                lax.fori_loop(0, width // size, level, 0)

        def leaf_down(i, carry):
            pieces = []
            for g in range(8):
                only = jnp.where(lane == g % 4, far_ref[i * 8 + g], 0.0)
                none = jnp.zeros((8, 128), F32)
                pieces.append(jnp.concatenate([only, none] if g < 4 else [none, only], axis=1))
            coefs = jnp.concatenate(pieces, axis=0).astype(BF16)
            basis = basis_ref[pl.ds(pl.multiple_of(i * 256, 256), 256), :]
            values = jnp.dot(coefs, basis, preferred_element_type=F32)
            for g in range(8):
                at = pl.ds(pl.multiple_of((i * 8 + g) * 128, 128), 128)
                out_ref[:, at] = out_ref[:, at] + values[8 * g : 8 * g + 8]
            return carry

        lax.fori_loop(0, leaves // 8, leaf_down, 0, unroll=4)
        for copy in halos + coef_halos + [copy for group in gathers for copy in group]:
            copy.wait_send()

    smem = pl.BlockSpec(memory_space=pltpu.SMEM)
    vmem = pl.BlockSpec(memory_space=pltpu.VMEM)
    hbm = pl.BlockSpec(memory_space=pl.ANY)
    n_copies = 6 + n_round
    return pl.pallas_call(
        kernel,
        out_shape=jax.ShapeDtypeStruct((8, length), F32),
        in_specs=[vmem] * 2 + [smem] + [hbm] * 7,
        out_specs=vmem,
        scratch_shapes=[
            pltpu.VMEM((near_slots, leaves), jnp.int32),
            pltpu.VMEM((slots, rows + 1), jnp.int32),
            pltpu.SMEM((near_slots, leaves), jnp.int32),
            pltpu.SMEM((slots, rows + 1), jnp.int32),
            pltpu.VMEM((3, length), F32),
            pltpu.VMEM((8, length), F32),
            pltpu.VMEM((leaves * 32, 128), BF16),
            pltpu.VMEM((rows - 1, 1024), BF16),
            pltpu.VMEM((rows + 1, slots, 1024), BF16),
            pltpu.VMEM((top_rows, 1024), BF16),
            pltpu.VMEM((branches - 2, top_slots, 1024), BF16),
            pltpu.VMEM((3, edge), F32),
            pltpu.VMEM((3, edge), F32),
            pltpu.VMEM((8, edge), F32),
            pltpu.VMEM((8, edge), F32),
            pltpu.VMEM((packs, 8, 128), F32),
            pltpu.VMEM((packs, 8, 128), F32),
            pltpu.VMEM((packs, 8, 128), F32),
            pltpu.VMEM((packs, 8, 128), F32),
            pltpu.VMEM((3 * rows + 1, 8, 128), F32),
            pltpu.VMEM((held[-1] + 1, 8, 128), F32),
            pltpu.VMEM((2, 8, 128), F32),
            pltpu.VMEM((rows + 1, 8, 128), F32),
            pltpu.VMEM((rows - 1, 1024), F32),
            pltpu.VMEM((top_rows, 1024), F32),
            pltpu.VMEM((span + 1, 32, 128), BF16),
            pltpu.VMEM((leaves, 32, 128), BF16),
            pltpu.VMEM((span + 1, 8, 128), F32),
            pltpu.VMEM((2, unroll, wide, 128), BF16),
            pltpu.VMEM((2, unroll, 8, wide), F32),
            pltpu.VMEM((chunk * slots, 1024), F32),
            pltpu.VMEM((8 * max(chunk, GROUP), 1024), F32),
            pltpu.VMEM((128, 1024), BF16),
            pltpu.VMEM((1024, 128), BF16),
            pltpu.SemaphoreType.DMA((9,)),
            pltpu.SemaphoreType.DMA((n_copies,)),
            pltpu.SemaphoreType.DMA((n_copies,)),
        ],
        compiler_params=pltpu.CompilerParams(
            vmem_limit_bytes=VMEM_BYTES, collective_id=0, has_side_effects=True
        ),
        cost_estimate=pl.CostEstimate(
            flops=4 * 10**10,
            bytes_accessed=16 << 20,
            transcendentals=leaves * near_slots * 128 * 128,
        ),
        name="product",
    )


def on_device(
    points,
    charges,
    leaf_basis,
    low_transfer,
    low_coupling,
    low_partner,
    top_transfer,
    top_coupling,
    top_partner,
    near_list,
):
    branches = lax.axis_size("branch")
    leaves = leaf_basis.shape[0]
    return make_product(
        leaves, branches, near_list.shape[1], low_partner.shape[1], top_partner.shape[1]
    )(
        near_list.T,
        low_partner.T,
        top_partner.T,
        points,
        charges,
        leaf_basis.reshape(leaves * 32, 128),
        low_transfer,
        low_coupling,
        top_transfer,
        top_coupling,
    )


def solution(mesh):
    return jax.shard_map(
        on_device,
        mesh=mesh,
        in_specs=(
            P(None, "branch"),
            P(None, "branch"),
            P("branch", None, None),
            P("branch", None),
            P("branch", None, None),
            P("branch", None),
            P(),
            P(),
            P(),
            P("branch", None),
        ),
        out_specs=P(None, "branch"),
        check_vma=False,
    )
```

```python
import math

import jax
import jax.numpy as jnp
from jax import lax
from jax.experimental import pallas as pl
from jax.experimental.pallas import tpu as pltpu
from jax.sharding import PartitionSpec as P

SOFTEN = 0.0025
FOURPI = 4.0 * math.pi
F32 = jnp.float32
BF16 = jnp.bfloat16
VMEM_BYTES = 60 << 20
GROUP = 128


def level_start(total, depth_at):
    return 2 * total - (2 * total >> depth_at)


def halo_counts(leaves, depth):
    return [max(1, (leaves // 4) >> k) for k in range(depth + 1)]


def lane_group(shape):
    return lax.broadcasted_iota(jnp.int32, shape, len(shape) - 1) // 32


def spread_groups(z):
    z = z + pltpu.roll(z, 32, axis=z.ndim - 1)
    return z + pltpu.roll(z, 64, axis=z.ndim - 1)


def expand_matrix():
    r = lax.broadcasted_iota(jnp.int32, (128, 1024), 0)
    c = lax.broadcasted_iota(jnp.int32, (128, 1024), 1)
    return jnp.where(((r % 32) == (c // 32)) & (r < 96), 1.0, 0.0).astype(BF16)


def reduce_matrix():
    r = lax.broadcasted_iota(jnp.int32, (1024, 128), 0)
    c = lax.broadcasted_iota(jnp.int32, (1024, 128), 1)
    return jnp.where((r // 32) == (c % 32), 1.0, 0.0).astype(BF16)


def expand(u, xmat):
    hi = u.astype(BF16).astype(F32)
    rest = u - hi
    mid = rest.astype(BF16).astype(F32)
    low = rest - mid
    group = lane_group(u.shape)
    parts = jnp.where(group == 0, hi, jnp.where(group == 1, mid, jnp.where(group == 2, low, 0.0)))
    return jnp.dot(parts.astype(BF16), xmat, preferred_element_type=F32)


def reduce32(acc, rmat):
    hi = acc.astype(BF16)
    low = (acc - hi.astype(F32)).astype(BF16)
    return jnp.dot(hi, rmat, preferred_element_type=F32) + jnp.dot(
        low, rmat, preferred_element_type=F32
    )


def point_rows(points):
    n = points.shape[1]
    row = lax.broadcasted_iota(jnp.int32, (8, n), 0)
    scaled = (points - 0.5) * FOURPI
    value = jnp.where(
        row == 0, scaled[0:1], jnp.where(row == 1, scaled[1:2], jnp.where(row == 2, scaled[2:3], 0.0))
    )
    high = value.astype(BF16).astype(F32)
    low = (value - high).astype(BF16).astype(F32)
    both = high + low
    norm = jnp.sum(both * both, axis=0, keepdims=True)
    return row, high, low, norm


def three_parts(norm):
    one = norm.astype(BF16).astype(F32)
    rest = norm - one
    two = rest.astype(BF16).astype(F32)
    return one, two, rest - two


def source_rows(row, high, low, norm):
    m1, m2, m3 = three_parts(norm)
    unit = row == 4
    s0 = jnp.where(row == 3, m1, jnp.where(unit, 1.0, high))
    s1 = jnp.where(row == 3, m2, jnp.where(unit, 1.0, low))
    s2 = jnp.where(row == 3, m3, jnp.where(unit, 1.0, high))
    return jnp.concatenate([s0, s1, s2, low], axis=0).astype(BF16)


def target_rows(row, high, low, norm):
    n1, n2, n3 = three_parts(norm + SOFTEN * FOURPI * FOURPI)
    unit = row == 3
    t0 = jnp.where(row == 4, n1, jnp.where(unit, 1.0, -2.0 * high))
    t1 = jnp.where(row == 4, n2, jnp.where(unit, 1.0, -2.0 * high))
    t2 = jnp.where(row == 4, n3, jnp.where(unit, 1.0, -2.0 * low))
    return jnp.concatenate([t0, t1, t2, -2.0 * low], axis=0).astype(BF16)


def spread_row(ref, at):
    return ref[pl.ds(at, 8, stride=0), :]


def move_up(u_ref, e_ref, xmat_ref, src, dst, e_row, width):
    group = min(GROUP, width)

    def step(i, carry):
        first = i * group
        mats = e_ref.at[pl.ds(pl.multiple_of(e_row + first, 8), group)] if group >= 8 else e_ref
        skip = 0 if group >= 8 else e_row
        u = u_ref[pl.ds(src + first, group)].reshape(group * 8, 128)
        wide = expand(u, xmat_ref[...])
        for n in range(0, group, 2):
            total = None
            for m in (n, n + 1):
                prod = wide[8 * m : 8 * m + 8] * spread_row(mats, skip + m)
                for j in range(8):
                    piece = prod[:, 128 * j : 128 * j + 128]
                    total = piece if total is None else total + piece
            u_ref[dst + i * (group // 2) + n // 2] = spread_groups(total)
        return carry

    if width == group:
        step(0, 0)
    else:
        lax.fori_loop(0, width // group, step, 0)


def upcast_rows(dst_ref, src_ref, rows):
    for first in range(0, rows, 64):
        count = min(64, rows - first)
        dst_ref[first : first + count, :] = src_ref[first : first + count, :].astype(F32)


def rounds_of(branches):
    rounds, stride = [], 1
    while stride < branches:
        size = 2 if stride == 1 or branches // stride == 2 else 4
        rounds.append((size, stride))
        stride *= size
    return rounds


def make_product(leaves, branches, near_slots, slots, top_slots):
    depth = leaves.bit_length() - 1
    depth_top = branches.bit_length() - 1
    counts = halo_counts(leaves, depth)
    packs = -(-sum(counts) // 4)
    rows = 2 * leaves - 1
    own = rows
    reach = leaves // 4
    span = leaves + 2 * reach
    edge = reach * 128
    length = leaves * 128
    unroll = 8
    chunk = 4 * unroll
    wide = near_slots * 128
    top_rows = 2 * branches - 4
    rounds = rounds_of(branches)
    n_round = sum(size - 1 for size, _ in rounds)
    loop_steps = leaves // (2 * unroll)
    held = [1]
    for r in range(1, len(rounds)):
        held.append(4 * held[-1] + sum(min(2, 3 - n) for n in (1, 2) if 2 * r + n - 1 < depth_top))

    def upper_row(level, node):
        r = level // 2
        bits = 1 if level % 2 == 0 else 0
        row = (4 * held[r - 1] if r else 0) + (node & 1 if bits else (2 if r else 0))
        block = node >> bits
        for i in range(r + 1, len(rounds)):
            row = row + (block & 3) * held[i - 1]
            block = block >> 2
        return row


    def kernel(
        near_list_ref,
        low_partner_ref,
        top_partner_ref,
        pts_hbm,
        chg_hbm,
        basis_hbm,
        transfer_hbm,
        coupling_hbm,
        top_transfer_hbm,
        top_coupling_hbm,
        out_ref,
        near_rows_ref,
        partner_rows_ref,
        index_ref,
        partner_ref,
        pts_ref,
        chg_ref,
        basis_ref,
        transfer_ref,
        coupling_ref,
        top_transfer_ref,
        top_coupling_ref,
        pts_before_ref,
        pts_after_ref,
        chg_before_ref,
        chg_after_ref,
        last_ref,
        first_ref,
        before_ref,
        after_ref,
        table_ref,
        upper_ref,
        roots_ref,
        far_ref,
        e_ref,
        top_e_ref,
        src_ref,
        tgt_ref,
        load_ref,
        tile_ref,
        rhs_ref,
        c_ref,
        acc_ref,
        xmat_ref,
        rmat_ref,
        load_sem,
        send_sem,
        recv_sem,
    ):
        me = lax.axis_index("branch")
        fetches = [
            pltpu.make_async_copy(a, b, load_sem.at[i])
            for i, (a, b) in enumerate(
                (
                    (chg_hbm, chg_ref),
                    (basis_hbm, basis_ref),
                    (transfer_hbm, transfer_ref),
                    (coupling_hbm, coupling_ref.at[0:rows]),
                    (pts_hbm, pts_ref),
                    (top_transfer_hbm, top_transfer_ref),
                    (top_coupling_hbm, top_coupling_ref),
                )
            )
        ]
        for fetch in fetches:
            fetch.start()

        right = (me + 1) % branches
        left = (me + branches - 1) % branches
        peers = []
        for size, stride in rounds:
            digit = (me // stride) % size
            for t in range(1, size):
                peers.append(me + ((digit + t) % size - digit) * stride)
        barrier = pltpu.get_barrier_semaphore()
        for other in [left, right] + peers:
            pl.semaphore_signal(
                barrier, inc=1, device_id=(other,), device_id_type=pl.DeviceIdType.MESH
            )

        def remote(i, a, b, other):
            return pltpu.make_async_remote_copy(
                src_ref=a,
                dst_ref=b,
                send_sem=send_sem.at[i],
                recv_sem=recv_sem.at[i],
                device_id=(other,),
                device_id_type=pl.DeviceIdType.MESH,
            )

        halos = [
            remote(0, pts_hbm.at[:, length - edge : length], pts_before_ref, right),
            remote(1, chg_hbm.at[:, length - edge : length], chg_before_ref, right),
            remote(2, pts_hbm.at[:, 0:edge], pts_after_ref, left),
            remote(3, chg_hbm.at[:, 0:edge], chg_after_ref, left),
        ]
        coef_halos = [
            remote(4, last_ref, before_ref, right),
            remote(5, first_ref, after_ref, left),
        ]
        digits = [(me // stride) % size for size, stride in rounds]
        gathers, at = [], 0
        for r, (size, stride) in enumerate(rounds):
            if r == 0:
                block = roots_ref.at[pl.ds(digits[0], 1)]
            else:
                first = sum(digits[i] * held[i - 1] for i in range(r, len(rounds)))
                block = upper_ref.at[pl.ds(first, held[r - 1])]
            gathers.append(
                [remote(6 + at + t, block, block, peers[at + t]) for t in range(size - 1)]
            )
            at += size - 1

        def lift(children, e_row):
            wide = expand(jnp.concatenate(children, axis=0), xmat_ref[...])
            parents = []
            for n in range(0, len(children), 2):
                total = None
                for m in (n, n + 1):
                    prod = wide[8 * m : 8 * m + 8] * top_e_ref[pl.ds(e_row + m, 1), :]
                    for j in range(8):
                        piece = prod[:, 128 * j : 128 * j + 128]
                        total = piece if total is None else total + piece
                parents.append(spread_groups(total))
            return parents

        def after_round(r):
            for copy in gathers[r]:
                copy.wait_recv()
            if r == 0:
                first = sum(digits[i] * held[i - 1] for i in range(1, len(rounds)))
                upper_ref[first] = lift([roots_ref[0], roots_ref[1]], (me // 2) * 2)[0]
                return
            size, stride = rounds[r]
            first = sum(digits[i] * held[i - 1] for i in range(r + 1, len(rounds)))
            block = me // (size * stride)
            level = 2 * r
            children = [upper_ref[first + n * held[r - 1] + held[r - 1] - 1] for n in range(4)]
            two = lift(children, level_start(branches, level - 1) + 4 * block)
            for n in range(2):
                upper_ref[first + 4 * held[r - 1] + n] = two[n]
            if level + 1 < depth_top:
                one = lift(two, level_start(branches, level) + 2 * block)
                upper_ref[first + 4 * held[r - 1] + 2] = one[0]


        entry = near_list_ref[...]
        near_rows_ref[...] = jnp.where(
            entry >= 0, jnp.maximum(entry - me * leaves + reach, 0), span
        )
        entry = low_partner_ref[...]
        partner_rows_ref[...] = jnp.full((slots, rows + 1), 3 * rows, jnp.int32)
        partner_rows_ref[:, 0:rows] = jnp.where(
            entry >= 0, jnp.maximum(entry - (me - 1) * rows, 0), 3 * rows
        )
        lists = [
            pltpu.make_async_copy(near_rows_ref, index_ref, load_sem.at[7]),
            pltpu.make_async_copy(partner_rows_ref, partner_ref, load_sem.at[8]),
        ]
        for copy in lists:
            copy.start()

        xmat_ref[...] = expand_matrix()
        rmat_ref[...] = reduce_matrix()

        fetches[0].wait()
        fetches[1].wait()

        def leaf_up(i, carry):
            at = pl.multiple_of(i * 1024, 1024)
            loads = chg_ref[:, pl.ds(at, 1024)]
            loads = jnp.concatenate([loads[:, 128 * g : 128 * g + 128] for g in range(8)], axis=0)
            basis = basis_ref[pl.ds(pl.multiple_of(i * 256, 256), 256), :]
            out = lax.dot_general(
                loads.astype(BF16), basis, (((1,), (1,)), ((), ())), preferred_element_type=F32
            )
            group = lane_group((8, 128))
            for g in range(8):
                piece = out[8 * g : 8 * g + 8, 128 * (g // 4) : 128 * (g // 4) + 128]
                table_ref[own + i * 8 + g] = spread_groups(jnp.where(group == g % 4, piece, 0.0))
            return carry

        lax.fori_loop(0, leaves // 8, leaf_up, 0, unroll=8)

        fetches[2].wait()
        upcast_rows(e_ref, transfer_ref, rows - 1)
        pl.semaphore_wait(barrier, 2 + len(peers))
        for copy in halos:
            copy.start()

        for k in range(depth):
            start = level_start(leaves, k)
            move_up(
                table_ref,
                e_ref,
                xmat_ref,
                own + start,
                own + level_start(leaves, k + 1),
                start,
                leaves >> k,
            )

        lane = lane_group((8, 128))
        for pack_ref, tail in ((last_ref, True), (first_ref, False)):
            nodes = []
            for k in range(depth + 1):
                start, width = level_start(leaves, k), leaves >> k
                begin = start + width - counts[k] if tail else start
                nodes += list(range(begin, begin + counts[k]))
            for at in range(0, len(nodes), 4):
                four = nodes[at : at + 4]
                packed = table_ref[own + four[0]]
                for g in range(1, len(four)):
                    packed = jnp.where(lane == g, table_ref[own + four[g]], packed)
                pack_ref[at // 4] = packed
        for copy in coef_halos:
            copy.start()
        roots_ref[pl.ds(digits[0], 1)] = table_ref[own + rows - 1 : own + rows]
        for copy in gathers[0]:
            copy.start()

        def prepare(points, charges, first, is_own, count):
            def step(i, carry):
                at = pl.multiple_of(i * 1024, 1024)
                parts = point_rows(points[:, pl.ds(at, 1024)])
                source = source_rows(*parts)
                loads = charges[:, pl.ds(at, 1024)]
                for g in range(8):
                    src_ref[first + i * 8 + g] = source[:, 128 * g : 128 * g + 128]
                    load_ref[first + i * 8 + g] = loads[:, 128 * g : 128 * g + 128]
                if is_own:
                    target = target_rows(*parts)
                    for g in range(8):
                        tgt_ref[i * 8 + g] = target[:, 128 * g : 128 * g + 128]
                return carry

            lax.fori_loop(0, count // 8, step, 0, unroll=4)

        fetches[4].wait()
        prepare(pts_ref, chg_ref, reach, True, leaves)
        for copy in halos:
            copy.wait_recv()
        prepare(pts_before_ref, chg_before_ref, 0, False, reach)
        prepare(pts_after_ref, chg_after_ref, reach + leaves, False, reach)
        src_ref[span] = src_ref[reach]
        load_ref[span] = jnp.zeros((8, 128), F32)

        def tiles_of(leaf, slot, j):
            target = tgt_ref[leaf]
            for s in range(near_slots):
                q = index_ref[s, leaf]
                square = lax.dot_general(
                    src_ref[q], target, (((0,), (0,)), ((), ())), preferred_element_type=F32
                )
                tile_ref[slot, j, 128 * s : 128 * s + 128, :] = lax.rsqrt(square).astype(BF16)
                rhs_ref[slot, j, :, 128 * s : 128 * s + 128] = load_ref[q]

        def apply(leaf, slot, j):
            at = pl.multiple_of(leaf * 128, 128)
            out_ref[:, pl.ds(at, 128)] = jnp.dot(
                rhs_ref[slot, j].astype(BF16), tile_ref[slot, j], preferred_element_type=F32
            )

        table_ref[3 * rows] = jnp.zeros((8, 128), F32)
        for copy in coef_halos:
            copy.wait_recv()
        for in_ref, tail, base in ((before_ref, True, 0), (after_ref, False, 2 * rows)):
            at = 0
            for k in range(depth + 1):
                start, width = level_start(leaves, k), leaves >> k
                begin = base + (start + width - counts[k] if tail else start)
                for i in range(counts[k]):
                    packed = in_ref[(at + i) // 4]
                    table_ref[begin + i] = spread_groups(
                        jnp.where(lane == (at + i) % 4, packed, 0.0)
                    )
                at += counts[k]

        coupling_ref[rows] = jnp.zeros((slots, 1024), BF16)
        fetches[3].wait()

        def couple(first, n):
            node = first + n
            acc = [None] * 8
            for s in range(slots):
                u = table_ref[partner_ref[s, node]]
                row = spread_row(c_ref, n * slots + s)
                for j in range(8):
                    piece = u * row[:, 128 * j : 128 * j + 128]
                    acc[j] = piece if acc[j] is None else acc[j] + piece
            for j in range(8):
                acc_ref[8 * n : 8 * n + 8, 128 * j : 128 * j + 128] = acc[j]

        fetches[5].wait()
        fetches[6].wait()
        upcast_rows(top_e_ref, top_transfer_ref, top_rows)
        for copy in lists:
            copy.wait()
        for j in range(unroll):
            tiles_of(j, 0, j)

        def near_step(i, carry):
            first = i * chunk
            c_ref[...] = coupling_ref[pl.ds(first, chunk)].reshape(chunk * slots, 1024).astype(F32)
            for half in range(2):
                base = (2 * i + half) * unroll
                for j in range(unroll):
                    tiles_of((base + unroll + j) % leaves, 1 - half, j)
                    for n in range(2):
                        couple(first, 2 * (half * unroll + j) + n)
                for j in range(unroll):
                    apply(base + j, half, j)
            far = jnp.dot(acc_ref[0 : 8 * chunk].astype(BF16), rmat_ref[...], preferred_element_type=F32)
            far_ref[pl.ds(first, chunk)] = far.reshape(chunk, 8, 128)
            for r in range(1, len(rounds)):

                @pl.when(i == (r * loop_steps) // (len(rounds) + 1))
                def _():
                    after_round(r - 1)
                    for copy in gathers[r]:
                        copy.start()

            return carry

        lax.fori_loop(0, loop_steps, near_step, 0)

        after_round(len(rounds) - 1)
        upper_ref[held[-1]] = jnp.zeros((8, 128), F32)
        for u in range(1, depth_top):
            row_at = level_start(branches, u) - branches + me // (1 << u)
            mats = top_coupling_ref[row_at].astype(F32)
            acc = [None] * 8
            for s in range(top_slots):
                entry = top_partner_ref[s, row_at]
                at = jnp.where(entry >= 0, upper_row(u, jnp.maximum(entry, 0)), held[-1])
                value = upper_ref[at]
                for j in range(8):
                    piece = value * mats[s : s + 1, 128 * j : 128 * j + 128]
                    acc[j] = piece if acc[j] is None else acc[j] + piece
            for j in range(8):
                acc_ref[8 * u - 8 : 8 * u, 128 * j : 128 * j + 128] = acc[j]
        far_top = reduce32(acc_ref[0 : 8 * (depth_top - 1)], rmat_ref[...])

        def down(value, row):
            return reduce32(jnp.concatenate([value] * 8, axis=1) * row, rmat_ref[...])

        current = far_top[8 * (depth_top - 2) :]
        for u in range(depth_top - 2, 0, -1):
            row = top_e_ref[pl.ds(level_start(branches, u) + me // (1 << u), 1), :]
            current = far_top[8 * u - 8 : 8 * u] + down(current, row)
        far_ref[rows - 1] = far_ref[rows - 1] + down(current, top_e_ref[pl.ds(me, 1), :])

        for k in range(depth - 1, -1, -1):
            start, width = level_start(leaves, k), leaves >> k
            parents = level_start(leaves, k + 1)
            size = min(GROUP, width)

            def level(i, carry, start=start, parents=parents, size=size):
                at = pl.multiple_of(start + i * size, 8) if size >= 8 else 0
                mats = e_ref.at[pl.ds(at, size)] if size >= 8 else e_ref
                skip = 0 if size >= 8 else start
                for n in range(size):
                    value = far_ref[parents + i * (size // 2) + n // 2]
                    row = spread_row(mats, skip + n)
                    for j in range(8):
                        acc_ref[8 * n : 8 * n + 8, 128 * j : 128 * j + 128] = (
                            value * row[:, 128 * j : 128 * j + 128]
                        )
                moved = reduce32(acc_ref[0 : 8 * size], rmat_ref[...])
                at = pl.ds(start + i * size, size)
                far_ref[at] = far_ref[at] + moved.reshape(size, 8, 128)
                return carry

            if width == size:
                level(0, 0)
            else:
                lax.fori_loop(0, width // size, level, 0)

        def leaf_down(i, carry):
            pieces = []
            for g in range(8):
                only = jnp.where(lane == g % 4, far_ref[i * 8 + g], 0.0)
                none = jnp.zeros((8, 128), F32)
                pieces.append(jnp.concatenate([only, none] if g < 4 else [none, only], axis=1))
            coefs = jnp.concatenate(pieces, axis=0).astype(BF16)
            basis = basis_ref[pl.ds(pl.multiple_of(i * 256, 256), 256), :]
            values = jnp.dot(coefs, basis, preferred_element_type=F32)
            for g in range(8):
                at = pl.ds(pl.multiple_of((i * 8 + g) * 128, 128), 128)
                out_ref[:, at] = out_ref[:, at] + values[8 * g : 8 * g + 8]
            return carry

        lax.fori_loop(0, leaves // 8, leaf_down, 0, unroll=8)
        for copy in halos + coef_halos + [copy for group in gathers for copy in group]:
            copy.wait_send()

    smem = pl.BlockSpec(memory_space=pltpu.SMEM)
    vmem = pl.BlockSpec(memory_space=pltpu.VMEM)
    hbm = pl.BlockSpec(memory_space=pl.ANY)
    n_copies = 6 + n_round
    return pl.pallas_call(
        kernel,
        out_shape=jax.ShapeDtypeStruct((8, length), F32),
        in_specs=[vmem] * 2 + [smem] + [hbm] * 7,
        out_specs=vmem,
        scratch_shapes=[
            pltpu.VMEM((near_slots, leaves), jnp.int32),
            pltpu.VMEM((slots, rows + 1), jnp.int32),
            pltpu.SMEM((near_slots, leaves), jnp.int32),
            pltpu.SMEM((slots, rows + 1), jnp.int32),
            pltpu.VMEM((3, length), F32),
            pltpu.VMEM((8, length), F32),
            pltpu.VMEM((leaves * 32, 128), BF16),
            pltpu.VMEM((rows - 1, 1024), BF16),
            pltpu.VMEM((rows + 1, slots, 1024), BF16),
            pltpu.VMEM((top_rows, 1024), BF16),
            pltpu.VMEM((branches - 2, top_slots, 1024), BF16),
            pltpu.VMEM((3, edge), F32),
            pltpu.VMEM((3, edge), F32),
            pltpu.VMEM((8, edge), F32),
            pltpu.VMEM((8, edge), F32),
            pltpu.VMEM((packs, 8, 128), F32),
            pltpu.VMEM((packs, 8, 128), F32),
            pltpu.VMEM((packs, 8, 128), F32),
            pltpu.VMEM((packs, 8, 128), F32),
            pltpu.VMEM((3 * rows + 1, 8, 128), F32),
            pltpu.VMEM((held[-1] + 1, 8, 128), F32),
            pltpu.VMEM((2, 8, 128), F32),
            pltpu.VMEM((rows + 1, 8, 128), F32),
            pltpu.VMEM((rows - 1, 1024), F32),
            pltpu.VMEM((top_rows, 1024), F32),
            pltpu.VMEM((span + 1, 32, 128), BF16),
            pltpu.VMEM((leaves, 32, 128), BF16),
            pltpu.VMEM((span + 1, 8, 128), F32),
            pltpu.VMEM((2, unroll, wide, 128), BF16),
            pltpu.VMEM((2, unroll, 8, wide), F32),
            pltpu.VMEM((chunk * slots, 1024), F32),
            pltpu.VMEM((8 * max(chunk, GROUP), 1024), F32),
            pltpu.VMEM((128, 1024), BF16),
            pltpu.VMEM((1024, 128), BF16),
            pltpu.SemaphoreType.DMA((9,)),
            pltpu.SemaphoreType.DMA((n_copies,)),
            pltpu.SemaphoreType.DMA((n_copies,)),
        ],
        compiler_params=pltpu.CompilerParams(
            vmem_limit_bytes=VMEM_BYTES, collective_id=0, has_side_effects=True
        ),
        cost_estimate=pl.CostEstimate(
            flops=4 * 10**10,
            bytes_accessed=16 << 20,
            transcendentals=leaves * near_slots * 128 * 128,
        ),
        name="product",
    )


def on_device(
    points,
    charges,
    leaf_basis,
    low_transfer,
    low_coupling,
    low_partner,
    top_transfer,
    top_coupling,
    top_partner,
    near_list,
):
    branches = lax.axis_size("branch")
    leaves = leaf_basis.shape[0]
    return make_product(
        leaves, branches, near_list.shape[1], low_partner.shape[1], top_partner.shape[1]
    )(
        near_list.T,
        low_partner.T,
        top_partner.T,
        points,
        charges,
        leaf_basis.reshape(leaves * 32, 128),
        low_transfer,
        low_coupling,
        top_transfer,
        top_coupling,
    )


def solution(mesh):
    return jax.shard_map(
        on_device,
        mesh=mesh,
        in_specs=(
            P(None, "branch"),
            P(None, "branch"),
            P("branch", None, None),
            P("branch", None),
            P("branch", None, None),
            P("branch", None),
            P(),
            P(),
            P(),
            P("branch", None),
        ),
        out_specs=P(None, "branch"),
        check_vma=False,
    )
```

```python
import math

import jax
import jax.numpy as jnp
from jax import lax
from jax.experimental import pallas as pl
from jax.experimental.pallas import tpu as pltpu
from jax.sharding import PartitionSpec as P

SOFTEN = 0.0025
FOURPI = 4.0 * math.pi
F32 = jnp.float32
BF16 = jnp.bfloat16
VMEM_BYTES = 60 << 20
GROUP = 128


def level_start(total, depth_at):
    return 2 * total - (2 * total >> depth_at)


def halo_counts(leaves, depth):
    return [max(1, (leaves // 4) >> k) for k in range(depth + 1)]


def lane_group(shape):
    return lax.broadcasted_iota(jnp.int32, shape, len(shape) - 1) // 32


def spread_groups(z):
    z = z + pltpu.roll(z, 32, axis=z.ndim - 1)
    return z + pltpu.roll(z, 64, axis=z.ndim - 1)


def expand_matrix():
    r = lax.broadcasted_iota(jnp.int32, (128, 1024), 0)
    c = lax.broadcasted_iota(jnp.int32, (128, 1024), 1)
    return jnp.where(((r % 32) == (c // 32)) & (r < 96), 1.0, 0.0).astype(BF16)


def reduce_matrix():
    r = lax.broadcasted_iota(jnp.int32, (1024, 128), 0)
    c = lax.broadcasted_iota(jnp.int32, (1024, 128), 1)
    return jnp.where((r // 32) == (c % 32), 1.0, 0.0).astype(BF16)


def expand(u, xmat):
    hi = u.astype(BF16).astype(F32)
    rest = u - hi
    mid = rest.astype(BF16).astype(F32)
    low = rest - mid
    group = lane_group(u.shape)
    parts = jnp.where(group == 0, hi, jnp.where(group == 1, mid, jnp.where(group == 2, low, 0.0)))
    return jnp.dot(parts.astype(BF16), xmat, preferred_element_type=F32)


def reduce32(acc, rmat):
    hi = acc.astype(BF16)
    low = (acc - hi.astype(F32)).astype(BF16)
    return jnp.dot(hi, rmat, preferred_element_type=F32) + jnp.dot(
        low, rmat, preferred_element_type=F32
    )


def point_rows(points):
    n = points.shape[1]
    row = lax.broadcasted_iota(jnp.int32, (8, n), 0)
    scaled = (points - 0.5) * FOURPI
    value = jnp.where(
        row == 0, scaled[0:1], jnp.where(row == 1, scaled[1:2], jnp.where(row == 2, scaled[2:3], 0.0))
    )
    high = value.astype(BF16).astype(F32)
    low = (value - high).astype(BF16).astype(F32)
    both = high + low
    norm = jnp.sum(both * both, axis=0, keepdims=True)
    return row, high, low, norm


def three_parts(norm):
    one = norm.astype(BF16).astype(F32)
    rest = norm - one
    two = rest.astype(BF16).astype(F32)
    return one, two, rest - two


def source_rows(row, high, low, norm):
    m1, m2, m3 = three_parts(norm)
    unit = row == 4
    s0 = jnp.where(row == 3, m1, jnp.where(unit, 1.0, high))
    s1 = jnp.where(row == 3, m2, jnp.where(unit, 1.0, low))
    s2 = jnp.where(row == 3, m3, jnp.where(unit, 1.0, high))
    return jnp.concatenate([s0, s1, s2, low], axis=0).astype(BF16)


def target_rows(row, high, low, norm):
    n1, n2, n3 = three_parts(norm + SOFTEN * FOURPI * FOURPI)
    unit = row == 3
    t0 = jnp.where(row == 4, n1, jnp.where(unit, 1.0, -2.0 * high))
    t1 = jnp.where(row == 4, n2, jnp.where(unit, 1.0, -2.0 * high))
    t2 = jnp.where(row == 4, n3, jnp.where(unit, 1.0, -2.0 * low))
    return jnp.concatenate([t0, t1, t2, -2.0 * low], axis=0).astype(BF16)


def spread_row(ref, at):
    return ref[pl.ds(at, 8, stride=0), :]


def move_up(u_ref, e_ref, xmat_ref, src, dst, e_row, width):
    group = min(GROUP, width)

    def step(i, carry):
        first = i * group
        mats = e_ref.at[pl.ds(pl.multiple_of(e_row + first, 8), group)] if group >= 8 else e_ref
        skip = 0 if group >= 8 else e_row
        u = u_ref[pl.ds(src + first, group)].reshape(group * 8, 128)
        wide = expand(u, xmat_ref[...])
        for n in range(0, group, 2):
            total = None
            for m in (n, n + 1):
                prod = wide[8 * m : 8 * m + 8] * spread_row(mats, skip + m)
                for j in range(8):
                    piece = prod[:, 128 * j : 128 * j + 128]
                    total = piece if total is None else total + piece
            u_ref[dst + i * (group // 2) + n // 2] = spread_groups(total)
        return carry

    if width == group:
        step(0, 0)
    else:
        lax.fori_loop(0, width // group, step, 0)


def upcast_rows(dst_ref, src_ref, rows):
    for first in range(0, rows, 64):
        count = min(64, rows - first)
        dst_ref[first : first + count, :] = src_ref[first : first + count, :].astype(F32)


def rounds_of(branches):
    rounds, stride = [], 1
    while stride < branches:
        size = 2 if stride == 1 or branches // stride == 2 else 4
        rounds.append((size, stride))
        stride *= size
    return rounds


def make_product(leaves, branches, near_slots, slots, top_slots):
    depth = leaves.bit_length() - 1
    depth_top = branches.bit_length() - 1
    counts = halo_counts(leaves, depth)
    packs = -(-sum(counts) // 4)
    rows = 2 * leaves - 1
    own = rows
    reach = leaves // 4
    span = leaves + 2 * reach
    edge = reach * 128
    length = leaves * 128
    unroll = 8
    chunk = 8 * unroll
    wide = near_slots * 128
    top_rows = 2 * branches - 4
    rounds = rounds_of(branches)
    n_round = sum(size - 1 for size, _ in rounds)
    inner = leaves - 2 * reach
    loop_steps = inner // (2 * unroll)
    starts = ((0, 5), (1, 1), (1, 4))
    held = [1]
    for r in range(1, len(rounds)):
        held.append(4 * held[-1] + sum(min(2, 3 - n) for n in (1, 2) if 2 * r + n - 1 < depth_top))

    def upper_row(level, node):
        r = level // 2
        bits = 1 if level % 2 == 0 else 0
        row = (4 * held[r - 1] if r else 0) + (node & 1 if bits else (2 if r else 0))
        block = node >> bits
        for i in range(r + 1, len(rounds)):
            row = row + (block & 3) * held[i - 1]
            block = block >> 2
        return row


    def kernel(
        near_list_ref,
        low_partner_ref,
        top_partner_ref,
        pts_hbm,
        chg_hbm,
        basis_hbm,
        transfer_hbm,
        coupling_hbm,
        top_transfer_hbm,
        top_coupling_hbm,
        out_ref,
        near_rows_ref,
        partner_rows_ref,
        index_ref,
        partner_ref,
        pts_ref,
        chg_ref,
        basis_ref,
        transfer_ref,
        coupling_ref,
        top_transfer_ref,
        top_coupling_ref,
        pts_before_ref,
        pts_after_ref,
        chg_before_ref,
        chg_after_ref,
        last_ref,
        first_ref,
        before_ref,
        after_ref,
        table_ref,
        upper_ref,
        roots_ref,
        far_ref,
        e_ref,
        top_e_ref,
        src_ref,
        own_src_ref,
        own_load_ref,
        tgt_ref,
        load_ref,
        tile_ref,
        rhs_ref,
        c_ref,
        acc_ref,
        xmat_ref,
        rmat_ref,
        load_sem,
        send_sem,
        recv_sem,
    ):
        me = lax.axis_index("branch")
        fetches = [
            pltpu.make_async_copy(a, b, load_sem.at[i])
            for i, (a, b) in enumerate(
                (
                    (chg_hbm, chg_ref),
                    (basis_hbm, basis_ref),
                    (transfer_hbm, transfer_ref),
                    (coupling_hbm, coupling_ref.at[0:rows]),
                    (pts_hbm, pts_ref),
                    (top_transfer_hbm, top_transfer_ref),
                    (top_coupling_hbm, top_coupling_ref),
                )
            )
        ]
        for fetch in fetches:
            fetch.start()

        right = (me + 1) % branches
        left = (me + branches - 1) % branches
        peers = []
        for size, stride in rounds:
            digit = (me // stride) % size
            for t in range(1, size):
                peers.append(me + ((digit + t) % size - digit) * stride)
        barrier = pltpu.get_barrier_semaphore()
        for other in [left, right] + peers:
            pl.semaphore_signal(
                barrier, inc=1, device_id=(other,), device_id_type=pl.DeviceIdType.MESH
            )

        def remote(i, a, b, other):
            return pltpu.make_async_remote_copy(
                src_ref=a,
                dst_ref=b,
                send_sem=send_sem.at[i],
                recv_sem=recv_sem.at[i],
                device_id=(other,),
                device_id_type=pl.DeviceIdType.MESH,
            )

        halos = [
            remote(0, pts_hbm.at[:, length - edge : length], pts_before_ref, right),
            remote(1, chg_hbm.at[:, length - edge : length], chg_before_ref, right),
            remote(2, pts_hbm.at[:, 0:edge], pts_after_ref, left),
            remote(3, chg_hbm.at[:, 0:edge], chg_after_ref, left),
        ]
        coef_halos = [
            remote(4, last_ref, before_ref, right),
            remote(5, first_ref, after_ref, left),
        ]
        digits = [(me // stride) % size for size, stride in rounds]
        gathers, at = [], 0
        for r, (size, stride) in enumerate(rounds):
            if r == 0:
                block = roots_ref.at[pl.ds(digits[0], 1)]
            else:
                first = sum(digits[i] * held[i - 1] for i in range(r, len(rounds)))
                block = upper_ref.at[pl.ds(first, held[r - 1])]
            gathers.append(
                [remote(6 + at + t, block, block, peers[at + t]) for t in range(size - 1)]
            )
            at += size - 1

        def lift(children, e_row):
            wide = expand(jnp.concatenate(children, axis=0), xmat_ref[...])
            parents = []
            for n in range(0, len(children), 2):
                total = None
                for m in (n, n + 1):
                    prod = wide[8 * m : 8 * m + 8] * top_e_ref[pl.ds(e_row + m, 1), :]
                    for j in range(8):
                        piece = prod[:, 128 * j : 128 * j + 128]
                        total = piece if total is None else total + piece
                parents.append(spread_groups(total))
            return parents

        def after_round(r):
            for copy in gathers[r]:
                copy.wait_recv()
            if r == 0:
                first = sum(digits[i] * held[i - 1] for i in range(1, len(rounds)))
                upper_ref[first] = lift([roots_ref[0], roots_ref[1]], (me // 2) * 2)[0]
                return
            size, stride = rounds[r]
            first = sum(digits[i] * held[i - 1] for i in range(r + 1, len(rounds)))
            block = me // (size * stride)
            level = 2 * r
            children = [upper_ref[first + n * held[r - 1] + held[r - 1] - 1] for n in range(4)]
            two = lift(children, level_start(branches, level - 1) + 4 * block)
            for n in range(2):
                upper_ref[first + 4 * held[r - 1] + n] = two[n]
            if level + 1 < depth_top:
                one = lift(two, level_start(branches, level) + 2 * block)
                upper_ref[first + 4 * held[r - 1] + 2] = one[0]


        entry = near_list_ref[...]
        leaf = lax.broadcasted_iota(jnp.int32, entry.shape, 1)
        alone = (leaf >= reach) & (leaf < leaves - reach)
        at = entry - me * leaves
        at = jnp.where(
            alone, jnp.clip(at, 0, leaves - 1), jnp.clip(at + reach, 0, span - 1)
        )
        near_rows_ref[...] = jnp.where(entry >= 0, at, jnp.where(alone, leaves, span))
        entry = low_partner_ref[...]
        partner_rows_ref[...] = jnp.full((slots, rows + 1), 3 * rows, jnp.int32)
        partner_rows_ref[:, 0:rows] = jnp.where(
            entry >= 0, jnp.maximum(entry - (me - 1) * rows, 0), 3 * rows
        )
        lists = [
            pltpu.make_async_copy(near_rows_ref, index_ref, load_sem.at[7]),
            pltpu.make_async_copy(partner_rows_ref, partner_ref, load_sem.at[8]),
        ]
        for copy in lists:
            copy.start()

        xmat_ref[...] = expand_matrix()
        rmat_ref[...] = reduce_matrix()

        fetches[0].wait()
        fetches[1].wait()

        def leaf_up(i, carry):
            at = pl.multiple_of(i * 1024, 1024)
            loads = chg_ref[:, pl.ds(at, 1024)]
            loads = jnp.concatenate([loads[:, 128 * g : 128 * g + 128] for g in range(8)], axis=0)
            basis = basis_ref[pl.ds(pl.multiple_of(i * 256, 256), 256), :]
            out = lax.dot_general(
                loads.astype(BF16), basis, (((1,), (1,)), ((), ())), preferred_element_type=F32
            )
            group = lane_group((8, 128))
            for g in range(8):
                piece = out[8 * g : 8 * g + 8, 128 * (g // 4) : 128 * (g // 4) + 128]
                table_ref[own + i * 8 + g] = spread_groups(jnp.where(group == g % 4, piece, 0.0))
            return carry

        lax.fori_loop(0, leaves // 8, leaf_up, 0, unroll=8)

        fetches[2].wait()
        upcast_rows(e_ref, transfer_ref, rows - 1)
        for k in range(depth):
            start = level_start(leaves, k)
            move_up(
                table_ref,
                e_ref,
                xmat_ref,
                own + start,
                own + level_start(leaves, k + 1),
                start,
                leaves >> k,
            )

        lane = lane_group((8, 128))
        for pack_ref, tail in ((last_ref, True), (first_ref, False)):
            nodes = []
            for k in range(depth + 1):
                start, width = level_start(leaves, k), leaves >> k
                begin = start + width - counts[k] if tail else start
                nodes += list(range(begin, begin + counts[k]))
            for at in range(0, len(nodes), 4):
                four = nodes[at : at + 4]
                packed = table_ref[own + four[0]]
                for g in range(1, len(four)):
                    packed = jnp.where(lane == g, table_ref[own + four[g]], packed)
                pack_ref[at // 4] = packed
        pl.semaphore_wait(barrier, 2 + len(peers))
        for copy in halos + coef_halos:
            copy.start()
        roots_ref[pl.ds(digits[0], 1)] = table_ref[own + rows - 1 : own + rows]
        for copy in gathers[0]:
            copy.start()

        def prepare(points, charges, first, is_own, count):
            def step(i, carry):
                at = pl.multiple_of(i * 1024, 1024)
                parts = point_rows(points[:, pl.ds(at, 1024)])
                source = source_rows(*parts)
                loads = charges[:, pl.ds(at, 1024)]
                for g in range(8):
                    src_ref[first + i * 8 + g] = source[:, 128 * g : 128 * g + 128]
                    load_ref[first + i * 8 + g] = loads[:, 128 * g : 128 * g + 128]
                if is_own:
                    target = target_rows(*parts)
                    for g in range(8):
                        own_src_ref[i * 8 + g] = source[:, 128 * g : 128 * g + 128]
                        own_load_ref[i * 8 + g] = loads[:, 128 * g : 128 * g + 128]
                        tgt_ref[i * 8 + g] = target[:, 128 * g : 128 * g + 128]
                return carry

            lax.fori_loop(0, count // 8, step, 0, unroll=4)

        fetches[4].wait()
        prepare(pts_ref, chg_ref, reach, True, leaves)
        own_src_ref[leaves] = own_src_ref[0]
        own_load_ref[leaves] = jnp.zeros((8, 128), F32)

        def tiles_of(leaf, slot, j, sources, charges):
            target = tgt_ref[leaf]
            for s in range(near_slots):
                q = index_ref[s, leaf]
                square = lax.dot_general(
                    sources[q], target, (((0,), (0,)), ((), ())), preferred_element_type=F32
                )
                tile_ref[slot, j, 128 * s : 128 * s + 128, :] = lax.rsqrt(square).astype(BF16)
                rhs_ref[slot, j, :, 128 * s : 128 * s + 128] = charges[q]

        def apply(leaf, slot, j):
            at = pl.multiple_of(leaf * 128, 128)
            out_ref[:, pl.ds(at, 128)] = jnp.dot(
                rhs_ref[slot, j].astype(BF16), tile_ref[slot, j], preferred_element_type=F32
            )

        fetches[5].wait()
        fetches[6].wait()
        upcast_rows(top_e_ref, top_transfer_ref, top_rows)
        for copy in lists:
            copy.wait()

        def start_rounds(part, i):
            for r in range(1, len(rounds)):
                if starts[r - 1][0] == part:

                    @pl.when(i == starts[r - 1][1])
                    def _():
                        after_round(r - 1)
                        for copy in gathers[r]:
                            copy.start()

        for j in range(unroll):
            tiles_of(reach + j, 0, j, own_src_ref, own_load_ref)

        def inner_step(i, carry):
            for half in range(2):
                base = (2 * i + half) * unroll
                for j in range(unroll):
                    leaf = reach + (base + unroll + j) % inner
                    tiles_of(leaf, 1 - half, j, own_src_ref, own_load_ref)
                for j in range(unroll):
                    apply(reach + base + j, half, j)
            start_rounds(0, i)
            return carry

        lax.fori_loop(0, loop_steps, inner_step, 0)

        for copy in halos:
            copy.wait_recv()
        prepare(pts_before_ref, chg_before_ref, 0, False, reach)
        prepare(pts_after_ref, chg_after_ref, reach + leaves, False, reach)
        src_ref[span] = src_ref[reach]
        load_ref[span] = jnp.zeros((8, 128), F32)

        table_ref[3 * rows] = jnp.zeros((8, 128), F32)
        for copy in coef_halos:
            copy.wait_recv()
        for in_ref, tail, base in ((before_ref, True, 0), (after_ref, False, 2 * rows)):
            at = 0
            for k in range(depth + 1):
                start, width = level_start(leaves, k), leaves >> k
                begin = base + (start + width - counts[k] if tail else start)
                for i in range(counts[k]):
                    packed = in_ref[(at + i) // 4]
                    table_ref[begin + i] = spread_groups(
                        jnp.where(lane == (at + i) % 4, packed, 0.0)
                    )
                at += counts[k]

        coupling_ref[rows] = jnp.zeros((slots, 1024), BF16)
        fetches[3].wait()

        def couple(first, n):
            node = first + n
            acc = [None] * 8
            for s in range(slots):
                u = table_ref[partner_ref[s, node]]
                row = spread_row(c_ref, n * slots + s)
                for j in range(8):
                    piece = u * row[:, 128 * j : 128 * j + 128]
                    acc[j] = piece if acc[j] is None else acc[j] + piece
            for j in range(8):
                acc_ref[8 * n : 8 * n + 8, 128 * j : 128 * j + 128] = acc[j]

        for j in range(unroll):
            tiles_of(leaves - reach + j, 0, j, src_ref, load_ref)

        def outer_step(i, carry):
            first = i * chunk
            c_ref[...] = coupling_ref[pl.ds(first, chunk)].reshape(chunk * slots, 1024).astype(F32)
            for half in range(2):
                base = leaves - reach + (2 * i + half) * unroll
                for j in range(unroll):
                    tiles_of((base + unroll + j) % leaves, 1 - half, j, src_ref, load_ref)
                    for n in range(4):
                        couple(first, 4 * (half * unroll + j) + n)
                for j in range(unroll):
                    apply((base + j) % leaves, half, j)
            far = jnp.dot(
                acc_ref[0 : 8 * chunk].astype(BF16), rmat_ref[...], preferred_element_type=F32
            )
            far_ref[pl.ds(first, chunk)] = far.reshape(chunk, 8, 128)
            start_rounds(1, i)
            return carry

        lax.fori_loop(0, loop_steps, outer_step, 0)

        after_round(len(rounds) - 1)
        upper_ref[held[-1]] = jnp.zeros((8, 128), F32)
        for u in range(1, depth_top):
            row_at = level_start(branches, u) - branches + me // (1 << u)
            mats = top_coupling_ref[row_at].astype(F32)
            acc = [None] * 8
            for s in range(top_slots):
                entry = top_partner_ref[s, row_at]
                at = jnp.where(entry >= 0, upper_row(u, jnp.maximum(entry, 0)), held[-1])
                value = upper_ref[at]
                for j in range(8):
                    piece = value * mats[s : s + 1, 128 * j : 128 * j + 128]
                    acc[j] = piece if acc[j] is None else acc[j] + piece
            for j in range(8):
                acc_ref[8 * u - 8 : 8 * u, 128 * j : 128 * j + 128] = acc[j]
        far_top = reduce32(acc_ref[0 : 8 * (depth_top - 1)], rmat_ref[...])

        def down(value, row):
            return reduce32(jnp.concatenate([value] * 8, axis=1) * row, rmat_ref[...])

        current = far_top[8 * (depth_top - 2) :]
        for u in range(depth_top - 2, 0, -1):
            row = top_e_ref[pl.ds(level_start(branches, u) + me // (1 << u), 1), :]
            current = far_top[8 * u - 8 : 8 * u] + down(current, row)
        far_ref[rows - 1] = far_ref[rows - 1] + down(current, top_e_ref[pl.ds(me, 1), :])

        for k in range(depth - 1, -1, -1):
            start, width = level_start(leaves, k), leaves >> k
            parents = level_start(leaves, k + 1)
            size = min(GROUP, width)

            def level(i, carry, start=start, parents=parents, size=size):
                at = pl.multiple_of(start + i * size, 8) if size >= 8 else 0
                mats = e_ref.at[pl.ds(at, size)] if size >= 8 else e_ref
                skip = 0 if size >= 8 else start
                for n in range(size):
                    value = far_ref[parents + i * (size // 2) + n // 2]
                    row = spread_row(mats, skip + n)
                    for j in range(8):
                        acc_ref[8 * n : 8 * n + 8, 128 * j : 128 * j + 128] = (
                            value * row[:, 128 * j : 128 * j + 128]
                        )
                moved = reduce32(acc_ref[0 : 8 * size], rmat_ref[...])
                at = pl.ds(start + i * size, size)
                far_ref[at] = far_ref[at] + moved.reshape(size, 8, 128)
                return carry

            if width == size:
                level(0, 0)
            else:
                lax.fori_loop(0, width // size, level, 0)

        def leaf_down(i, carry):
            pieces = []
            for g in range(8):
                only = jnp.where(lane == g % 4, far_ref[i * 8 + g], 0.0)
                none = jnp.zeros((8, 128), F32)
                pieces.append(jnp.concatenate([only, none] if g < 4 else [none, only], axis=1))
            coefs = jnp.concatenate(pieces, axis=0).astype(BF16)
            basis = basis_ref[pl.ds(pl.multiple_of(i * 256, 256), 256), :]
            values = jnp.dot(coefs, basis, preferred_element_type=F32)
            for g in range(8):
                at = pl.ds(pl.multiple_of((i * 8 + g) * 128, 128), 128)
                out_ref[:, at] = out_ref[:, at] + values[8 * g : 8 * g + 8]
            return carry

        lax.fori_loop(0, leaves // 8, leaf_down, 0, unroll=8)
        for copy in halos + coef_halos + [copy for group in gathers for copy in group]:
            copy.wait_send()

    smem = pl.BlockSpec(memory_space=pltpu.SMEM)
    vmem = pl.BlockSpec(memory_space=pltpu.VMEM)
    hbm = pl.BlockSpec(memory_space=pl.ANY)
    n_copies = 6 + n_round
    return pl.pallas_call(
        kernel,
        out_shape=jax.ShapeDtypeStruct((8, length), F32),
        in_specs=[vmem] * 2 + [smem] + [hbm] * 7,
        out_specs=vmem,
        scratch_shapes=[
            pltpu.VMEM((near_slots, leaves), jnp.int32),
            pltpu.VMEM((slots, rows + 1), jnp.int32),
            pltpu.SMEM((near_slots, leaves), jnp.int32),
            pltpu.SMEM((slots, rows + 1), jnp.int32),
            pltpu.VMEM((3, length), F32),
            pltpu.VMEM((8, length), F32),
            pltpu.VMEM((leaves * 32, 128), BF16),
            pltpu.VMEM((rows - 1, 1024), BF16),
            pltpu.VMEM((rows + 1, slots, 1024), BF16),
            pltpu.VMEM((top_rows, 1024), BF16),
            pltpu.VMEM((branches - 2, top_slots, 1024), BF16),
            pltpu.VMEM((3, edge), F32),
            pltpu.VMEM((3, edge), F32),
            pltpu.VMEM((8, edge), F32),
            pltpu.VMEM((8, edge), F32),
            pltpu.VMEM((packs, 8, 128), F32),
            pltpu.VMEM((packs, 8, 128), F32),
            pltpu.VMEM((packs, 8, 128), F32),
            pltpu.VMEM((packs, 8, 128), F32),
            pltpu.VMEM((3 * rows + 1, 8, 128), F32),
            pltpu.VMEM((held[-1] + 1, 8, 128), F32),
            pltpu.VMEM((2, 8, 128), F32),
            pltpu.VMEM((rows + 1, 8, 128), F32),
            pltpu.VMEM((rows - 1, 1024), F32),
            pltpu.VMEM((top_rows, 1024), F32),
            pltpu.VMEM((span + 1, 32, 128), BF16),
            pltpu.VMEM((leaves + 1, 32, 128), BF16),
            pltpu.VMEM((leaves + 1, 8, 128), F32),
            pltpu.VMEM((leaves, 32, 128), BF16),
            pltpu.VMEM((span + 1, 8, 128), F32),
            pltpu.VMEM((2, unroll, wide, 128), BF16),
            pltpu.VMEM((2, unroll, 8, wide), F32),
            pltpu.VMEM((chunk * slots, 1024), F32),
            pltpu.VMEM((8 * max(chunk, GROUP), 1024), F32),
            pltpu.VMEM((128, 1024), BF16),
            pltpu.VMEM((1024, 128), BF16),
            pltpu.SemaphoreType.DMA((9,)),
            pltpu.SemaphoreType.DMA((n_copies,)),
            pltpu.SemaphoreType.DMA((n_copies,)),
        ],
        compiler_params=pltpu.CompilerParams(
            vmem_limit_bytes=VMEM_BYTES, collective_id=0, has_side_effects=True
        ),
        cost_estimate=pl.CostEstimate(
            flops=4 * 10**10,
            bytes_accessed=16 << 20,
            transcendentals=leaves * near_slots * 128 * 128,
        ),
        name="product",
    )


def on_device(
    points,
    charges,
    leaf_basis,
    low_transfer,
    low_coupling,
    low_partner,
    top_transfer,
    top_coupling,
    top_partner,
    near_list,
):
    branches = lax.axis_size("branch")
    leaves = leaf_basis.shape[0]
    return make_product(
        leaves, branches, near_list.shape[1], low_partner.shape[1], top_partner.shape[1]
    )(
        near_list.T,
        low_partner.T,
        top_partner.T,
        points,
        charges,
        leaf_basis.reshape(leaves * 32, 128),
        low_transfer,
        low_coupling,
        top_transfer,
        top_coupling,
    )


def solution(mesh):
    return jax.shard_map(
        on_device,
        mesh=mesh,
        in_specs=(
            P(None, "branch"),
            P(None, "branch"),
            P("branch", None, None),
            P("branch", None),
            P("branch", None, None),
            P("branch", None),
            P(),
            P(),
            P(),
            P("branch", None),
        ),
        out_specs=P(None, "branch"),
        check_vma=False,
    )
```
